128 devices in a mesh: dp: 16 (over x, y), seq: 8 (over z, core).
Axes of the slice: x: 4, y: 4, z: 4, core: 2. Of those that a mesh axis runs over, the one named last changes fastest.
Arguments:
- img_qkv: bfloat16 [16, 1024, 7680], P('dp', 'seq'), may hold values from -20 to 20
- text_cache: bfloat16 [128, 333, 2432], P('dp', None, 'seq'), may hold values from -6 to 6
- null_rows: bfloat16 [333, 2432], P(None, 'seq'), may hold values from -6 to 6
- w_text: bfloat16 [2432, 7680], P(None, 'seq'), may hold values from -0.125 to 0.125
- cache_owner: int32 [16], replicated, may hold values from 0 to 15, as said below
- cache_row: int32 [16], replicated, may hold values from 0 to 7
- dropped: int32 [16, 2], replicated, may hold values from 0 to 1, as said below
- text_length: int32 [16], replicated, may hold values from 78 to 333, as said below
- d_img_out: bfloat16 [16, 1024, 2560], P('dp', 'seq'), may hold values from -6 to 6
- d_text_out: bfloat16 [16, 333, 2560], P('dp', None, 'seq'), may hold values from -6 to 6
Outputs:
- img_out: bfloat16 [16, 1024, 2560], P('dp', 'seq')
- text_out: bfloat16 [16, 333, 2560], P('dp', None, 'seq')
- d_img_qkv: bfloat16 [16, 1024, 7680], P('dp', 'seq')
- d_w_text: float32 [2432, 7680], P('dp', 'seq')
The draws below stay inside these ranges and needn't reach their ends.
Inputs may be any that keep to these rules, and one draw needn't show every extreme that they name: cache_owner is a permutation: every index of dp owns the caption of exactly one sample. No sample has both parts dropped. `text_length`: some sample has the length 333.
All inputs are finite; a program needn't handle non-finite values.
Results may differ from the reference program's by a relative error of at most 0.012.
The reference program's roundings to bfloat16 on the way count: a program that leaves them out, or rounds other values in their place, can miss the bound.
Values may be sent and summed in bfloat16 or wider, within the bound.
A program may use at most 128 MiB of HBM per device.

```python
import jax
import jax.numpy as jnp
from jax import lax

D = 2432
HEADS = 40
HD = 64
TXT = 333
CLIP = 77
CACHE_DEV = 8
BATCH = 16
IMG = 1024
CACHE = 128
N_DP = 16


def draw_img_qkv(key, part):
    key = jax.random.fold_in(key, 11)
    shape = (BATCH, IMG, HEADS, 3, HD)
    values = jnp.clip(jax.random.normal(key, shape, jnp.float32), -6.0, 6.0)
    return values.reshape(BATCH, IMG, HEADS * 3 * HD).astype(jnp.bfloat16)


def draw_cache_owner(key, part):
    key = jax.random.fold_in(key, 12)
    return jax.random.permutation(key, N_DP).astype(jnp.int32)


def draw_dropped(key, part):
    key = jax.random.fold_in(key, 13)
    ticket = jax.random.randint(key, (BATCH,), 0, 10)
    chosen = jax.random.permutation(jax.random.fold_in(key, 1), BATCH)
    ticket = ticket.at[chosen[0]].set(0).at[chosen[1]].set(2)
    clip_drop = (ticket < 2).astype(jnp.int32)
    t5_drop = ((ticket >= 2) & (ticket < 4)).astype(jnp.int32)
    return jnp.stack([clip_drop, t5_drop], axis=1)


def draw_text_length(key, part):
    key = jax.random.fold_in(key, 14)
    lengths = jax.random.randint(key, (BATCH,), CLIP + 1, TXT + 1)
    chosen = jax.random.randint(jax.random.fold_in(key, 1), (), 0, BATCH)
    return jnp.where(jnp.arange(BATCH) == chosen, TXT, lengths).astype(jnp.int32)


def with_ends(drawn, own_key, low, largest):
    dims = drawn.shape
    index_at = [jax.random.randint(jax.random.fold_in(own_key, axis), (), 0, dims[axis]) for axis in range(len(dims))]
    drawn = drawn.at[tuple(index_at)].set(low)
    longest = dims.index(max(dims))
    index_at[longest] = (index_at[longest] + 1) % dims[longest]
    return drawn.at[tuple(index_at)].set(largest)


def level_of(rng, dims, shards, low, largest):
    level = 1.0
    for position, parts in shards:
        heights = jax.random.uniform(jax.random.fold_in(jax.random.fold_in(rng, 6), position), (parts,), jnp.float32, low / len(shards), largest / len(shards))
        level = level * jnp.repeat(jnp.exp(heights), dims[position] // parts).reshape((-1,) + (1,) * (len(dims) - 1 - position))
    return level


def noise(stream_key, extent, deviation, most, shards=(), dtype=jnp.bfloat16):
    values = deviation * jax.random.normal(stream_key, extent, jnp.float32)
    if shards:
        values = values * level_of(stream_key, extent, shards, -0.22, 0.18)
    return jnp.clip(values, -most, most).astype(dtype)


def setup_inputs(seed: int = 0) -> dict:
    splits = jax.random.split(jax.random.key(seed), 11)
    img_qkv = draw_img_qkv(jax.random.fold_in(splits[10], 71), 0)
    text_cache = noise(splits[1], (CACHE, TXT, D), 1.0, 6.0, ((0, 16), (2, 8)))
    null_rows = noise(splits[2], (TXT, D), 1.0, 6.0, ((1, 8),))
    w_text = noise(splits[3], (D, HEADS * 3 * HD), D ** -0.5, 0.125, ((1, 8),))
    cache_owner = draw_cache_owner(jax.random.fold_in(splits[10], 71), 0)
    cache_row = with_ends(jax.random.randint(splits[5], (BATCH,), 0, CACHE_DEV), jax.random.fold_in(splits[5], 1), 0, CACHE_DEV - 1).astype(jnp.int32)
    dropped = draw_dropped(jax.random.fold_in(splits[10], 71), 0)
    text_length = draw_text_length(jax.random.fold_in(splits[10], 71), 0)
    d_img_out = noise(splits[8], (BATCH, IMG, HEADS * HD), 1.0, 6.0, ((0, 16), (1, 8)))
    d_text_out = noise(splits[9], (BATCH, TXT, HEADS * HD), 1.0, 6.0, ((0, 16), (2, 8)))
    return dict(img_qkv=img_qkv, text_cache=text_cache, null_rows=null_rows, w_text=w_text, cache_owner=cache_owner, cache_row=cache_row, dropped=dropped, text_length=text_length, d_img_out=d_img_out, d_text_out=d_text_out)


def reference(img_qkv, text_cache, null_rows, w_text, cache_owner, cache_row, dropped, text_length, d_img_out, d_text_out):
    softmax_scale = HD ** -0.5
    flat_index = (cache_owner * CACHE_DEV + cache_row).astype(jnp.int32)
    fetched = jnp.take(text_cache, flat_index, axis=0)
    t5_part = jnp.arange(TXT) >= CLIP
    drop_here = jnp.where(t5_part[None, :], dropped[:, 1:2], dropped[:, 0:1]) == 1
    text_rows = jnp.where(drop_here[:, :, None], null_rows[None], fetched)
    flat_rows = text_rows.reshape(BATCH * TXT, D)
    text_qkv = jnp.dot(flat_rows, w_text, preferred_element_type=jnp.float32).astype(jnp.bfloat16)
    text_qkv = text_qkv.reshape(BATCH, TXT, HEADS, 3, HD)
    image = img_qkv.reshape(BATCH, IMG, HEADS, 3, HD)
    total_len = IMG + TXT
    joint_qkv = jnp.concatenate([image, text_qkv], axis=1)
    joint_qkv = joint_qkv.transpose(0, 2, 1, 3, 4).reshape(BATCH * HEADS, total_len, 3, HD)
    visible = jnp.concatenate([jnp.ones((BATCH, IMG), bool), jnp.arange(TXT)[None, :] < text_length[:, None]], axis=1)
    visible = jnp.repeat(visible, HEADS, axis=0)
    upstream = jnp.concatenate([d_img_out.reshape(BATCH, IMG, HEADS, HD), d_text_out.reshape(BATCH, TXT, HEADS, HD)], axis=1)
    upstream = upstream.transpose(0, 2, 1, 3).reshape(BATCH * HEADS, total_len, HD)

    def per_head(inputs):
        packed, seen, cotangent = inputs
        queries = packed[:, 0]
        keys_here = packed[:, 1]
        values_here = packed[:, 2]
        scores = jnp.dot(queries, keys_here.T, preferred_element_type=jnp.float32) * softmax_scale
        scores = jnp.where(seen[None, :], scores, -jnp.inf)
        row_max = jnp.max(scores, axis=1, keepdims=True)
        exp_scores = jnp.exp(scores - row_max)
        attn_probs = (exp_scores / jnp.sum(exp_scores, axis=1, keepdims=True)).astype(jnp.bfloat16)
        attended = jnp.dot(attn_probs, values_here, preferred_element_type=jnp.float32).astype(jnp.bfloat16)
        d_values = jnp.dot(attn_probs.T, cotangent, preferred_element_type=jnp.float32).astype(jnp.bfloat16)
        d_probs = jnp.dot(cotangent, values_here.T, preferred_element_type=jnp.float32)
        row_delta = jnp.sum(cotangent.astype(jnp.float32) * attended.astype(jnp.float32), axis=1, keepdims=True)
        d_scores = (attn_probs.astype(jnp.float32) * (d_probs - row_delta) * softmax_scale).astype(jnp.bfloat16)
        d_queries = jnp.dot(d_scores, keys_here, preferred_element_type=jnp.float32).astype(jnp.bfloat16)
        d_keys = jnp.dot(d_scores.T, queries, preferred_element_type=jnp.float32).astype(jnp.bfloat16)
        return attended, jnp.stack([d_queries, d_keys, d_values], axis=1)

    attended, d_joint = lax.map(per_head, (joint_qkv, visible, upstream))
    attended = attended.reshape(BATCH, HEADS, total_len, HD).transpose(0, 2, 1, 3)
    img_out = attended[:, :IMG].reshape(BATCH, IMG, HEADS * HD)
    text_out = attended[:, IMG:].reshape(BATCH, TXT, HEADS * HD)
    d_joint = d_joint.reshape(BATCH, HEADS, total_len, 3, HD).transpose(0, 2, 1, 3, 4)
    d_img_qkv = d_joint[:, :IMG].reshape(BATCH, IMG, HEADS * 3 * HD)
    d_text_qkv = d_joint[:, IMG:].reshape(BATCH * TXT, HEADS * 3 * HD)
    d_w_text = jnp.dot(flat_rows.T, d_text_qkv, preferred_element_type=jnp.float32)
    return img_out, text_out, d_img_qkv, d_w_text
```

```python
import functools

import jax
import jax.numpy as jnp
from jax import lax
from jax.experimental import pallas as pl
from jax.experimental.pallas import tpu as pltpu
from jax.sharding import PartitionSpec as P

HD = 64
CLIP = 77
BQ = 256
KC = 272
f32, bf16 = jnp.float32, jnp.bfloat16


def chunks(n, c):
    return [(s, min(c, n - s)) for s in range(0, n, c)]


def dot(a, b):
    return jnp.dot(a, b, preferred_element_type=f32)


def fold(x, op):
    parts = [x[8 * i : 8 * i + 8] for i in range(x.shape[0] // 8)]
    while len(parts) > 1:
        parts = [
            op(parts[j], parts[j + 1]) if j + 1 < len(parts) else parts[j]
            for j in range(0, len(parts), 2)
        ]
    return parts[0]


def query_block(i, img, nk, x, xt, bias, s_scr, e_scr, acc, out):
    q0 = pl.multiple_of(i * BQ, BQ)
    zeros = jnp.zeros((HD, BQ), bf16)
    q_t = xt[0:64, pl.ds(q0, BQ)] * bf16(0.125)
    cot_t = xt[192:256, pl.ds(q0, BQ)].astype(f32)
    w_scores = jnp.concatenate([zeros, q_t], 0)
    top8 = None
    for k, n in chunks(nk, KC):
        s = dot(x[k : k + n, 0:128], w_scores)
        if k + n > img:
            b = bias[max(k - img, 0) : k + n - img, :]
            b = jnp.concatenate([b] * (BQ // 128), 1)
            s = s + b if k >= img else jnp.concatenate([s[: img - k], s[img - k :] + b], 0)
        s_scr[k : k + n, :] = s
        c = fold(s, jnp.maximum)
        top8 = c if top8 is None else jnp.maximum(top8, c)
    top = jnp.max(top8, 0, keepdims=True)
    sum8 = out_t = None
    for k, n in chunks(nk, KC):
        e = jnp.exp(s_scr[k : k + n, :] - top)
        c = fold(e, jnp.add)
        sum8 = c if sum8 is None else sum8 + c
        e = e.astype(bf16)
        e_scr[k : k + n, :] = e
        o = dot(xt[128:192, k : k + n], e)
        out_t = o if out_t is None else out_t + o
    inv = 1.0 / jnp.sum(sum8, 0, keepdims=True)
    out_t = (out_t * inv).astype(bf16)
    delta = jnp.sum(cot_t * out_t.astype(f32), 0, keepdims=True) * inv
    cot_s = (cot_t * inv).astype(bf16)
    w_probs = jnp.concatenate([cot_s, zeros], 0)
    w_values = jnp.concatenate([zeros, cot_s], 0).T
    w_keys = jnp.concatenate([q_t, zeros], 0).T
    dq_t = None
    for k, n in chunks(nk, KC):
        dp = dot(x[k : k + n, 128:256], w_probs)
        e = e_scr[k : k + n, :]
        ds = (e.astype(f32) * (dp - delta)).astype(bf16)
        d = dot(xt[64:128, k : k + n], ds)
        dq_t = d if dq_t is None else dq_t + d
        acc[k : k + n, :] += dot(ds, w_keys) + dot(e, w_values)
    dq_t = (dq_t * 0.125).astype(bf16)
    out[pl.ds(q0, BQ), 0:128] = jnp.concatenate([dq_t, out_t], 0).T


def swap_halves(v):
    return jnp.concatenate([v[:, HD:], v[:, :HD]], 1)


def low_lanes(shape):
    return lax.broadcasted_iota(jnp.int32, shape, 1) < HD


def split_pair(t0, t1, t2, cot):
    low = low_lanes(t0.shape)
    r1, r2, rc = swap_halves(t1), swap_halves(t2), swap_halves(cot)
    return (t0, jnp.where(low, t1, rc)), (jnp.where(low, r1, r2), jnp.where(low, r2, cot))


def join_pair(a0, b0, a1, b1):
    low = low_lanes(a0.shape)
    ra0, rb0, ra1 = swap_halves(a0), swap_halves(b0), swap_halves(a1)
    return (
        jnp.where(low, a0, rb0),
        jnp.where(low, rb0, ra1),
        b1,
        jnp.where(low, ra0, a1),
    )


def tiles_of(rows, lanes):
    return [(r, c) for r in range(0, rows, 16) for c in range(0, lanes, 128)]


GROUPS = ((1, (0, 256), (256, 384)), (3, (384, 512), (512, 768)), (4, (768, 896), (896, 1024)))


def kernel(
    dims,
    qkv,
    cot_img,
    cache,
    null_rows,
    w_hbm,
    owner,
    cache_row,
    dropped,
    length,
    cot_text,
    img_out,
    text_out,
    d_qkv,
    d_w,
    packed,
    x_all,
    out_all,
    back,
    w_text,
    rows_all,
    rows_t,
    text_qkv,
    text_cot,
    raw,
    null_pad,
    pieces,
    pieces_in,
    pieces_out,
    pieces_got,
    d_text,
    term,
    term_in,
    part,
    part_in,
    bias,
    xt,
    s_scr,
    e_scr,
    acc,
    sem_w,
    sems_a,
    sems_b,
    sems_c,
    sems_f,
    sems_in,
    sems_out,
    sems_1,
    sems_2,
):
    n_dp, n_seq, nx, ny = dims
    dp, me = lax.axis_index("dp"), lax.axis_index("seq")
    mx, my = dp // ny, dp % ny
    tokens = qkv.shape[0]
    heads = x_all.shape[0]
    nq = x_all.shape[1]
    img = tokens * n_seq
    nk = e_scr.shape[0]
    txt_pad = nk - img
    txt, depth = null_rows.shape
    lanes = raw.shape[1]
    per = pieces.shape[1]
    chunk_rows = d_w.shape[0]

    def remote(src, dst, sems, at, dev):
        return pltpu.make_async_remote_copy(
            src_ref=src,
            dst_ref=dst,
            send_sem=sems.at[(0,) + at],
            recv_sem=sems.at[(1,) + at],
            device_id=dev,
            device_id_type=pl.DeviceIdType.MESH,
        )

    def each(n, fn, start=0):
        def body(i, c):
            fn(i)
            return c

        lax.fori_loop(start, n, body, 0)

    barrier = pltpu.get_barrier_semaphore()

    def greet_seq(o):
        pl.semaphore_signal(
            barrier, inc=1, device_id=(dp, me ^ o), device_id_type=pl.DeviceIdType.MESH
        )

    def greet_dp(o):
        pl.semaphore_signal(
            barrier, inc=1, device_id=(dp ^ o, me), device_id_type=pl.DeviceIdType.MESH
        )

    each(n_seq, greet_seq, 1)
    each(n_dp, greet_dp, 1)
    w_copy = pltpu.make_async_copy(w_hbm, w_text, sem_w)
    w_copy.start()

    mine = jnp.int32(0)
    for b in range(n_dp):
        mine = jnp.where(owner[b] == dp, jnp.int32(b), mine)
    row = cache_row[mine]
    raw[...] = jnp.zeros_like(raw)
    raw[0:txt, 0:depth] = cache[row]
    null_pad[...] = jnp.zeros_like(null_pad)
    null_pad[0:txt, 0:depth] = null_rows[...]
    tiles = tiles_of(txt_pad, lanes)
    for t, (r, c) in enumerate(tiles):
        pieces[t // per, t % per] = raw[r : r + 16, c : c + 128]
    for t in range(len(tiles), n_dp * per):
        pieces[t // per, t % per] = jnp.zeros((16, 128), bf16)
    pieces_in[dp] = pieces[dp]

    pl.semaphore_wait(barrier, n_seq + n_dp - 2)

    def send_a(o):
        return remote(pieces.at[dp ^ o], pieces_in.at[dp], sems_a, (o,), (dp ^ o, me))

    def recv_a(o):
        return remote(pieces.at[dp], pieces_in.at[dp ^ o], sems_a, (o,), (dp ^ o, me))

    each(n_dp, lambda o: send_a(o).start(), 1)

    def pack(p):
        c = pl.multiple_of(p * 384, 128)
        t = [qkv[:, pl.ds(pl.multiple_of(c + 128 * j, 128), 128)] for j in range(3)]
        g = cot_img[:, pl.ds(pl.multiple_of(p * 128, 128), 128)]
        for j, (a, b) in enumerate(split_pair(*t, g)):
            head = 2 * p + j
            to, h = head // heads, head % heads
            packed[to, h, :, 0:128] = a
            packed[to, h, :, 128:256] = b

    each(n_seq * heads // 2, pack)
    mine_rows = pl.ds(pl.multiple_of(me * tokens, tokens), tokens)

    def peer_rows(o):
        return pl.ds(pl.multiple_of((me ^ o) * tokens, tokens), tokens)

    def send_in(h, o):
        return remote(
            packed.at[me ^ o, h], x_all.at[h, mine_rows], sems_in, (h, o), (dp, me ^ o)
        )

    def recv_in(h, o):
        return remote(
            packed.at[me, h], x_all.at[h, peer_rows(o)], sems_in, (h, o), (dp, me ^ o)
        )

    each(n_seq, lambda o: send_in(0, o).start(), 1)

    each(n_dp, lambda o: recv_a(o).wait_recv(), 1)
    for b in range(n_dp):
        pieces_out[b] = pieces_in[owner[b]]

    def send_b(o):
        return remote(pieces_out.at[dp ^ o], pieces_got.at[dp], sems_b, (o,), (dp ^ o, me))

    def recv_b(o):
        return remote(pieces_out.at[dp], pieces_got.at[dp ^ o], sems_b, (o,), (dp ^ o, me))

    each(n_dp, lambda o: send_b(o).start(), 1)
    pieces_got[dp] = pieces_out[dp]
    each(n_seq, lambda o: send_in(1, o).start(), 1)

    def own_image(h):
        x_all[h, mine_rows, :] = packed[me, h]
        x_all[h, nk:nq, :] = jnp.zeros((nq - nk, 256), bf16)

    each(heads, own_image)
    rows_all[:, txt_pad:, :] = jnp.zeros((n_seq, rows_all.shape[1] - txt_pad, lanes), bf16)
    text_cot[...] = jnp.zeros_like(text_cot)
    text_cot[0:txt, 0 : cot_text.shape[1]] = cot_text[...]
    seen = lax.broadcasted_iota(jnp.int32, bias.shape, 0) < length[dp]
    bias[...] = jnp.where(seen, 0.0, -1e30)
    drop_clip, drop_t5 = dropped[dp, 0], dropped[dp, 1]

    each(n_dp, lambda o: recv_b(o).wait_recv(), 1)
    for t, (r, c) in enumerate(tiles):
        got = pieces_got[t // per, t % per].astype(f32)
        token = lax.broadcasted_iota(jnp.int32, (16, 128), 0) + r
        drop = jnp.where(token < CLIP, drop_clip, drop_t5)
        own = null_pad[r : r + 16, c : c + 128].astype(f32)
        rows_all[me, r : r + 16, c : c + 128] = jnp.where(drop == 1, own, got).astype(bf16)

    def block(s):
        return rows_all.at[s, pl.ds(0, txt_pad)]

    def send_c(o):
        return remote(block(me), block(me), sems_c, (o,), (dp, me ^ o))

    def recv_c(o):
        return remote(block(me), block(me ^ o), sems_c, (o,), (dp, me ^ o))

    def send_f(o):
        return remote(block(me ^ o), block(me ^ o), sems_f, (o,), (dp, me ^ 1))

    def recv_f(o):
        return remote(block(me ^ 1), block(me ^ 1 ^ o), sems_f, (o,), (dp, me ^ 1))

    far = list(range(2, n_seq, 2))
    for o in far + [1]:
        send_c(o).start()
    for h in range(2, heads):
        each(n_seq, lambda o: send_in(h, o).start(), 1)
    for o in far:
        recv_c(o).wait_recv()
        send_f(o).start()
    recv_c(1).wait_recv()
    for o in far:
        recv_f(o).wait_recv()
    w_copy.wait()

    width = w_text.shape[1]
    for c, n in chunks(width, 256):
        total = None
        for s in range(n_seq):
            d = dot(rows_all[s, 0:txt_pad, 0:depth], w_text[s * depth : (s + 1) * depth, c : c + n])
            total = d if total is None else total + d
        text_qkv[:, c : c + n] = total.astype(bf16)
    for p in range((heads + 1) // 2):
        t = [text_qkv[:, 384 * p + 128 * j : 384 * p + 128 * j + 128] for j in range(2)]
        g = text_cot[:, 128 * p : 128 * p + 128]
        last = 2 * p + 1 == heads
        t.append(t[0] if last else text_qkv[:, 384 * p + 256 : 384 * p + 384])
        for j, (a, b) in enumerate(split_pair(*t, g)):
            if 2 * p + j < heads:
                x_all[2 * p + j, img:nk, 0:128] = a
                x_all[2 * p + j, img:nk, 128:256] = b

    def turn(s):
        v = rows_all[s].astype(f32).T
        for j in range(depth // chunk_rows):
            i = s * (depth // chunk_rows) + j
            v_j = v[j * chunk_rows : j * chunk_rows + rows_t.shape[1], :]
            rows_t[i] = v_j.astype(bf16)

    each(n_seq, turn)

    def send_out(h, o):
        return remote(
            out_all.at[h, peer_rows(o)], back.at[h, me], sems_out, (h, o), (dp, me ^ o)
        )

    def recv_out(h, o):
        return remote(
            out_all.at[h, mine_rows], back.at[h, me ^ o], sems_out, (h, o), (dp, me ^ o)
        )

    def ranges(g, side):
        lo, hi = GROUPS[g][1 + side]
        return pl.ds(lo, hi - lo)

    def along(side, o):
        return (mx * ny + (my ^ o), me) if side == 0 else ((mx ^ o) * ny + my, me)

    def first(g, side, o, sending):
        here = my if side == 0 else mx
        other = here ^ o
        to = other if sending else here
        lane = ranges(g, side)
        src = term.at[:, to, :, lane] if side == 0 else term.at[to, :, :, lane]
        slot = here if sending else other
        return remote(
            src, term_in.at[side, slot, :, :, lane], sems_1, (g, side, o), along(side, o)
        )

    def second(g, side, o, sending):
        here = mx if side == 0 else my
        other = here ^ o
        lane = ranges(g, side)
        to = other if sending else here
        slot = here if sending else other
        return remote(
            part.at[to, :, lane],
            part_in.at[slot, :, lane],
            sems_2,
            (g, side, o),
            along(1 - side, o),
        )

    def finish_heads(g):
        last = GROUPS[g][0]
        lo, hi = GROUPS[g][1][0], GROUPS[g][2][1]
        p = g
        o0, o1 = 2 * p, min(2 * p + 1, heads - 1)
        v = [out_all[h, img:nk, c : c + 128] for h in (o0, o1) for c in (0, 128)]
        j = join_pair(*v)
        if last % 2:
            for i in range(3):
                d_text[:, lo + 128 * i : lo + 128 * i + 128] = j[i]
            text_out[:, 128 * p : 128 * p + 128] = j[3][0:txt]
        else:
            low = low_lanes(j[1].shape)
            d_text[:, lo : lo + 128] = j[0]
            d_text[:, lo + 128 : lo + 256] = jnp.where(low, j[1], jnp.zeros_like(j[1]))
            text_out[:, 128 * p : 128 * p + HD] = j[3][0:txt, 0:HD]

        def multiply(x):
            a = rows_t[pl.ds(x * ny, ny)].reshape(ny * rows_t.shape[1], rows_t.shape[2])
            d = dot(a[:, 0:txt_pad], d_text[:, lo:hi]).astype(bf16)
            term[x, :, :, lo:hi] = d.reshape(ny, rows_t.shape[1], hi - lo)

        each(nx, multiply)
        for side in range(2):
            for o in range(1, ny if side == 0 else nx):
                first(g, side, o, True).start()

    def add_first(g):
        for side in range(2):
            k = ny if side == 0 else nx
            for o in range(1, k):
                first(g, side, o, False).wait_recv()
            here = my if side == 0 else mx
            lane = ranges(g, side)

            def add(j):
                own = term[j, here, :, lane] if side == 0 else term[here, j, :, lane]
                total = own.astype(f32)
                for o in range(1, k):
                    total = total + term_in[side, here ^ o, j, :, lane].astype(f32)
                part[j, :, lane] = total.astype(bf16)

            n = nx if side == 0 else ny
            each(n, add)
            for o in range(1, n):
                second(g, side, o, True).start()

    def add_second(g):
        for side in range(2):
            n = nx if side == 0 else ny
            for o in range(1, n):
                second(g, side, o, False).wait_recv()
            here = mx if side == 0 else my
            lane = ranges(g, side)
            total = part[here, :, lane].astype(f32)
            for o in range(1, n):
                total = total + part_in[here ^ o, :, lane].astype(f32)
            size = min(lane.start + lane.size, d_w.shape[1]) - lane.start
            d_w[:, lane.start : lane.start + size] = total[0:chunk_rows, 0:size]

    def one_head(h):
        each(n_seq, lambda o: recv_in(h, o).wait_recv(), 1)
        x, out = x_all.at[h], out_all.at[h]
        acc[...] = jnp.zeros_like(acc)
        for r in range(0, nq, BQ):
            xt[:, r : r + BQ] = x[r : r + BQ, :].T
        each(
            nq // BQ,
            lambda i: query_block(i, img, nk, x, xt, bias, s_scr, e_scr, acc, out),
        )
        for k, n in chunks(nk, KC):
            out[k : k + n, 128:256] = acc[k : k + n, :].astype(bf16)
        each(n_seq, lambda o: send_out(h, o).start(), 1)
        back[h, me] = out[mine_rows, :]
        for g in range(len(GROUPS)):
            pl.when(h == GROUPS[g][0])(functools.partial(finish_heads, g))
            if g + 1 < len(GROUPS):
                pl.when(h == GROUPS[g][0] + 1)(functools.partial(add_first, g))

    each(heads, one_head)

    for g in range(len(GROUPS) - 1):
        add_second(g)
    for h in range(heads):
        each(n_seq, lambda o: recv_out(h, o).wait_recv(), 1)

    def unpack(p):
        v = []
        for j in range(2):
            head = 2 * p + j
            s, h = head // heads, head % heads
            v += [back[h, s, :, 0:128], back[h, s, :, 128:256]]
        t = join_pair(*v)
        for j in range(3):
            d_qkv[:, pl.ds(pl.multiple_of(p * 384 + 128 * j, 128), 128)] = t[j]
        img_out[:, pl.ds(pl.multiple_of(p * 128, 128), 128)] = t[3]

    each(n_seq * heads // 2, unpack)
    add_first(len(GROUPS) - 1)
    add_second(len(GROUPS) - 1)

    each(n_dp, lambda o: send_a(o).wait_send(), 1)
    each(n_dp, lambda o: send_b(o).wait_send(), 1)
    for o in far + [1]:
        send_c(o).wait_send()
    for o in far:
        send_f(o).wait_send()
    for h in range(heads):
        each(n_seq, lambda o: send_in(h, o).wait_send(), 1)
        each(n_seq, lambda o: send_out(h, o).wait_send(), 1)
    for g in range(len(GROUPS)):
        for side in range(2):
            for o in range(1, ny if side == 0 else nx):
                first(g, side, o, True).wait_send()
            for o in range(1, nx if side == 0 else ny):
                second(g, side, o, True).wait_send()


def on_device(
    img_qkv,
    text_cache,
    null_rows,
    w_text,
    cache_owner,
    cache_row,
    dropped,
    text_length,
    d_img_out,
    d_text_out,
):
    n_dp, n_seq = lax.axis_size("dp"), lax.axis_size("seq")
    ny = 4
    nx = n_dp // ny
    txt, depth = null_rows.shape
    tokens = img_qkv.shape[1]
    width = w_text.shape[1]
    heads = width // (3 * HD)
    img = tokens * n_seq
    nk = -(-(img + txt) // 16) * 16
    nq = -(-(img + txt) // BQ) * BQ
    txt_pad = nk - img
    lanes = -(-depth // 128) * 128
    per = -(-(txt_pad // 16 * (lanes // 128)) // n_dp)
    chunk_rows = depth * n_seq // n_dp
    chunk_pad = -(-chunk_rows // 16) * 16
    wide = -(-width // 128) * 128
    rows_pad = -(-txt_pad // 128) * 128
    vmem = pl.BlockSpec(memory_space=pltpu.VMEM)
    smem = pl.BlockSpec(memory_space=pltpu.SMEM)
    dma = pltpu.SemaphoreType.DMA
    out_shape = (
        jax.ShapeDtypeStruct((tokens, n_seq * heads * HD), bf16),
        jax.ShapeDtypeStruct((txt, heads * HD), bf16),
        jax.ShapeDtypeStruct((tokens, n_seq * width), bf16),
        jax.ShapeDtypeStruct((chunk_rows, width), f32),
    )
    scratch = [
        pltpu.VMEM((n_seq, heads, tokens, 256), bf16),
        pltpu.VMEM((heads, nq, 256), bf16),
        pltpu.VMEM((heads, nq, 256), bf16),
        pltpu.VMEM((heads, n_seq, tokens, 256), bf16),
        pltpu.VMEM(w_text.shape, bf16),
        pltpu.VMEM((n_seq, rows_pad, lanes), bf16),
        pltpu.VMEM((n_dp, chunk_pad, rows_pad), bf16),
        pltpu.VMEM((txt_pad, wide), bf16),
        pltpu.VMEM((txt_pad, -(-heads // 2) * 128), bf16),
        pltpu.VMEM((txt_pad, lanes), bf16),
        pltpu.VMEM((txt_pad, lanes), bf16),
        pltpu.VMEM((n_dp, per, 16, 128), bf16),
        pltpu.VMEM((n_dp, per, 16, 128), bf16),
        pltpu.VMEM((n_dp, per, 16, 128), bf16),
        pltpu.VMEM((n_dp, per, 16, 128), bf16),
        pltpu.VMEM((txt_pad, wide), bf16),
        pltpu.VMEM((nx, ny, chunk_pad, wide), bf16),
        pltpu.VMEM((2, ny, nx, chunk_pad, wide), bf16),
        pltpu.VMEM((nx, chunk_pad, wide), bf16),
        pltpu.VMEM((nx, chunk_pad, wide), bf16),
        pltpu.VMEM((txt_pad, 128), f32),
        pltpu.VMEM((256, nq), bf16),
        pltpu.VMEM((nk, BQ), f32),
        pltpu.VMEM((nk, BQ), bf16),
        pltpu.VMEM((nk, 128), f32),
        dma,
        dma((2, n_dp)),
        dma((2, n_dp)),
        dma((2, n_seq)),
        dma((2, n_seq)),
        dma((2, heads, n_seq)),
        dma((2, heads, n_seq)),
        dma((2, len(GROUPS), 2, max(nx, ny))),
        dma((2, len(GROUPS), 2, max(nx, ny))),
    ]
    img_out, text_out, d_qkv, d_w = pl.pallas_call(
        functools.partial(kernel, (n_dp, n_seq, nx, ny)),
        out_shape=out_shape,
        in_specs=[vmem, vmem, vmem, vmem, pl.BlockSpec(memory_space=pl.ANY)]
        + [smem] * 4
        + [vmem],
        out_specs=(vmem,) * 4,
        scratch_shapes=scratch,
        compiler_params=pltpu.CompilerParams(
            collective_id=0, has_side_effects=True, vmem_limit_bytes=62 * 2**20
        ),
    )(
        img_qkv[0],
        d_img_out[0],
        text_cache,
        null_rows,
        w_text,
        cache_owner,
        cache_row,
        dropped,
        text_length,
        d_text_out[0],
    )
    return (img_out[None], text_out[None], d_qkv[None], d_w)


def solution(mesh):
    return jax.shard_map(
        on_device,
        mesh=mesh,
        in_specs=(
            P("dp", "seq", None),
            P("dp", None, "seq"),
            P(None, "seq"),
            P(None, "seq"),
            P(),
            P(),
            P(),
            P(),
            P("dp", "seq", None),
            P("dp", None, "seq"),
        ),
        out_specs=(
            P("dp", "seq", None),
            P("dp", None, "seq"),
            P("dp", "seq", None),
            P("dp", "seq"),
        ),
        check_vma=False,
    )
```

```python
import functools

import jax
import jax.numpy as jnp
from jax import lax
from jax.experimental import pallas as pl
from jax.experimental.pallas import tpu as pltpu
from jax.sharding import PartitionSpec as P

HD = 64
CLIP = 77
BQ = 256
KC = 464
f32, bf16 = jnp.float32, jnp.bfloat16


def chunks(n, c):
    return [(s, min(c, n - s)) for s in range(0, n, c)]


def dot(a, b):
    return jnp.dot(a, b, preferred_element_type=f32)


def fold(x, op):
    parts = [x[8 * i : 8 * i + 8] for i in range(x.shape[0] // 8)]
    while len(parts) > 1:
        parts = [
            op(parts[j], parts[j + 1]) if j + 1 < len(parts) else parts[j]
            for j in range(0, len(parts), 2)
        ]
    return parts[0]


def forward_block(i, img, nk, x, xt, bias, s_scr, e_scr, state):
    w_probs, w_values, w_keys, delta, attended = state
    q0 = pl.multiple_of(i * BQ, BQ)
    zeros = jnp.zeros((HD, BQ), bf16)
    q_t = xt[0:64, pl.ds(q0, BQ)] * bf16(0.125)
    w_scores = jnp.concatenate([zeros, q_t], 0)
    top8 = None
    for k, n in chunks(nk, KC):
        s = dot(x[k : k + n, 0:128], w_scores)
        if k + n > img:
            b = bias[max(k - img, 0) : k + n - img, :]
            b = jnp.concatenate([b] * (BQ // 128), 1)
            s = s + b if k >= img else jnp.concatenate([s[: img - k], s[img - k :] + b], 0)
        s_scr[k : k + n, :] = s
        c = fold(s, jnp.maximum)
        top8 = c if top8 is None else jnp.maximum(top8, c)
        yield
    top = jnp.max(top8, 0, keepdims=True)
    sum8 = out_t = None
    for k, n in chunks(nk, KC):
        e = jnp.exp(s_scr[k : k + n, :] - top)
        c = fold(e, jnp.add)
        sum8 = c if sum8 is None else sum8 + c
        e = e.astype(bf16)
        e_scr[k : k + n, :] = e
        o = dot(xt[128:192, k : k + n], e)
        out_t = o if out_t is None else out_t + o
        yield
    cot_t = xt[192:256, pl.ds(q0, BQ)].astype(f32)
    inv = 1.0 / jnp.sum(sum8, 0, keepdims=True)
    out_t = (out_t * inv).astype(bf16)
    row_delta = jnp.sum(cot_t * out_t.astype(f32), 0, keepdims=True) * inv
    cot_s = (cot_t * inv).astype(bf16)
    w_probs[...] = jnp.concatenate([cot_s, zeros], 0)
    w_values[...] = jnp.concatenate([zeros, cot_s], 0).T
    w_keys[...] = jnp.concatenate([q_t, zeros], 0).T
    delta[...] = jnp.broadcast_to(row_delta, delta.shape)
    attended[...] = out_t


def backward_block(i, nk, x, xt, e_scr, state, acc, out, attended_t):
    w_probs, w_values, w_keys, delta, attended = state
    q0 = pl.multiple_of(i * BQ, BQ)
    row_delta = delta[0:1, :]
    dq_t = None
    for k, n in chunks(nk, KC):
        dp = dot(x[k : k + n, 128:256], w_probs[...])
        e = e_scr[k : k + n, :]
        ds = (e.astype(f32) * (dp - row_delta)).astype(bf16)
        d = dot(xt[64:128, k : k + n], ds)
        dq_t = d if dq_t is None else dq_t + d
        acc[k : k + n, :] += dot(ds, w_keys[...]) + dot(e, w_values[...])
        yield
    dq_t = (dq_t * 0.125).astype(bf16)
    out[pl.ds(q0, BQ), 0:128] = jnp.concatenate([dq_t, attended[...]], 0).T
    attended_t[:, pl.ds(q0, BQ)] = attended[...]


def alternate(a, b):
    live = [True, True]
    turn = 0
    while live[0] or live[1]:
        g = 1 if turn % 3 == 2 else 0
        turn += 1
        if live[g]:
            live[g] = next((a, b)[g], "end") is None


def all_blocks(n, img, nk, x, xt, bias, s_scr, e_scrs, states, acc, out, attended_t):
    def forward(i, side):
        return forward_block(i, img, nk, x, xt, bias, s_scr, e_scrs[side], states[side])

    def backward(i, side):
        return backward_block(i, nk, x, xt, e_scrs[side], states[side], acc, out, attended_t)

    for _ in forward(0, 0):
        pass

    def body(j, c):
        alternate(forward(2 * j + 1, 1), backward(2 * j, 0))
        alternate(forward(2 * j + 2, 0), backward(2 * j + 1, 1))
        return c

    lax.fori_loop(0, (n - 1) // 2, body, 0)
    if n % 2 == 0:
        alternate(forward(n - 1, 1), backward(n - 2, 0))
    for _ in backward(n - 1, (n - 1) % 2):
        pass


def swap_halves(v):
    return jnp.concatenate([v[:, HD:], v[:, :HD]], 1)


def low_lanes(shape):
    return lax.broadcasted_iota(jnp.int32, shape, 1) < HD


def split_pair(t0, t1, t2, cot):
    low = low_lanes(t0.shape)
    r1, r2, rc = swap_halves(t1), swap_halves(t2), swap_halves(cot)
    return (t0, jnp.where(low, t1, rc)), (jnp.where(low, r1, r2), jnp.where(low, r2, cot))


def join_pair(a0, b0, a1, b1):
    low = low_lanes(a0.shape)
    ra0, rb0, ra1 = swap_halves(a0), swap_halves(b0), swap_halves(a1)
    return (
        jnp.where(low, a0, rb0),
        jnp.where(low, rb0, ra1),
        b1,
        jnp.where(low, ra0, a1),
    )


def tiles_of(rows, lanes):
    return [(r, c) for r in range(0, rows, 16) for c in range(0, lanes, 128)]


GROUPS = (
    ((0, 128), None),
    ((128, 256), (256, 384)),
    (None, (384, 512)),
    ((512, 640), (640, 768)),
    ((768, 896), (896, 1024)),
)


def kernel(
    dims,
    qkv,
    cot_img,
    cache,
    null_rows,
    w_hbm,
    owner,
    cache_row,
    dropped,
    length,
    cot_text,
    back,
    text_out,
    d_w,
    packed,
    x_all,
    out_all,
    attended_t,
    w_t,
    rows_t,
    text_cot,
    raw,
    null_pad,
    pieces,
    pieces_in,
    pieces_out,
    pieces_got,
    d_text,
    term,
    term_in,
    part,
    part_in,
    bias,
    xt,
    s_scr,
    e_scr0,
    e_scr1,
    acc,
    st_a0,
    st_a1,
    st_b0,
    st_b1,
    st_c0,
    st_c1,
    st_d0,
    st_d1,
    st_e0,
    st_e1,
    sem_w,
    sems_a,
    sems_b,
    sems_c,
    sems_f,
    sems_in,
    sems_out,
    sems_1,
    sems_2,
):
    n_dp, n_seq, nx, ny = dims
    dp, me = lax.axis_index("dp"), lax.axis_index("seq")
    mx, my = dp // ny, dp % ny
    tokens = qkv.shape[0]
    heads = x_all.shape[0]
    nq = xt.shape[1]
    n_x = x_all.shape[1]
    img = tokens * n_seq
    nk = e_scr0.shape[0]
    e_scrs = (e_scr0, e_scr1)
    states = ((st_a0, st_b0, st_c0, st_d0, st_e0), (st_a1, st_b1, st_c1, st_d1, st_e1))
    txt_pad = nk - img
    depth, txt = null_rows.shape
    lanes = raw.shape[1]
    per = pieces.shape[1]
    chunk_rows = d_w.shape[0]

    def remote(src, dst, sems, at, dev):
        return pltpu.make_async_remote_copy(
            src_ref=src,
            dst_ref=dst,
            send_sem=sems.at[(0,) + at],
            recv_sem=sems.at[(1,) + at],
            device_id=dev,
            device_id_type=pl.DeviceIdType.MESH,
        )

    def each(n, fn, start=0):
        def body(i, c):
            fn(i)
            return c

        lax.fori_loop(start, n, body, 0)

    barrier = pltpu.get_barrier_semaphore()

    def greet_seq(o):
        pl.semaphore_signal(
            barrier, inc=1, device_id=(dp, me ^ o), device_id_type=pl.DeviceIdType.MESH
        )

    def greet_dp(o):
        pl.semaphore_signal(
            barrier, inc=1, device_id=(dp ^ o, me), device_id_type=pl.DeviceIdType.MESH
        )

    each(n_seq, greet_seq, 1)
    each(n_dp, greet_dp, 1)
    w_copy = pltpu.make_async_copy(w_hbm, w_t, sem_w)
    w_copy.start()

    mine = jnp.int32(0)
    for b in range(n_dp):
        mine = jnp.where(owner[b] == dp, jnp.int32(b), mine)
    row = cache_row[mine]
    raw[...] = jnp.zeros_like(raw)
    raw[:, 0:txt] = cache[row]
    null_pad[...] = jnp.zeros_like(null_pad)
    null_pad[:, 0:txt] = null_rows[...]
    tiles = tiles_of(depth, lanes)
    for t, (r, c) in enumerate(tiles):
        pieces[t // per, t % per] = raw[r : r + 16, c : c + 128]
    for t in range(len(tiles), n_dp * per):
        pieces[t // per, t % per] = jnp.zeros((16, 128), bf16)
    pieces_in[dp] = pieces[dp]

    def pack(p):
        c = pl.multiple_of(p * 384, 128)
        t = [qkv[:, pl.ds(pl.multiple_of(c + 128 * j, 128), 128)] for j in range(3)]
        g = cot_img[:, pl.ds(pl.multiple_of(p * 128, 128), 128)]
        for j, (a, b) in enumerate(split_pair(*t, g)):
            head = 2 * p + j
            to, h = head // heads, head % heads
            packed[to, h, :, 0:128] = a
            packed[to, h, :, 128:256] = b

    lax.fori_loop(0, n_seq, lambda i, c: (pack(i * heads // 2), c)[1], 0, unroll=2)

    pl.semaphore_wait(barrier, n_seq + n_dp - 2)

    def send_a(o):
        return remote(pieces.at[dp ^ o], pieces_in.at[dp], sems_a, (o,), (dp ^ o, me))

    def recv_a(o):
        return remote(pieces.at[dp], pieces_in.at[dp ^ o], sems_a, (o,), (dp ^ o, me))

    each(n_dp, lambda o: send_a(o).start(), 1)

    mine_rows = pl.ds(pl.multiple_of(me * tokens, tokens), tokens)

    def peer_rows(o):
        return pl.ds(pl.multiple_of((me ^ o) * tokens, tokens), tokens)

    def send_in(h, o):
        return remote(
            packed.at[me ^ o, h], x_all.at[h, mine_rows], sems_in, (h, o), (dp, me ^ o)
        )

    def recv_in(h, o):
        return remote(
            packed.at[me, h], x_all.at[h, peer_rows(o)], sems_in, (h, o), (dp, me ^ o)
        )

    each(n_seq, lambda o: send_in(0, o).start(), 1)

    def pack_rest(i):
        for j in (1, 3, 4):
            pack(i * heads + j)

    each(n_seq // 2, pack_rest)

    each(n_dp, lambda o: recv_a(o).wait_recv(), 1)
    for b in range(n_dp):
        pieces_out[b] = pieces_in[owner[b]]

    def send_b(o):
        return remote(pieces_out.at[dp ^ o], pieces_got.at[dp], sems_b, (o,), (dp ^ o, me))

    def recv_b(o):
        return remote(pieces_out.at[dp], pieces_got.at[dp ^ o], sems_b, (o,), (dp ^ o, me))

    each(n_dp, lambda o: send_b(o).start(), 1)
    pieces_got[dp] = pieces_out[dp]

    def own_image(h):
        x_all[h, mine_rows, :] = packed[me, h]

    each(heads, own_image)
    text_cot[...] = jnp.zeros_like(text_cot)
    text_cot[:, 0:txt] = cot_text[...]
    if nq > n_x:
        xt[:, n_x:nq] = jnp.zeros((256, nq - n_x), bf16)
    seen = lax.broadcasted_iota(jnp.int32, bias.shape, 0) < length[dp]
    bias[...] = jnp.where(seen, 0.0, -1e30)
    drop_clip, drop_t5 = dropped[0, dp], dropped[1, dp]

    each(n_dp, lambda o: recv_b(o).wait_recv(), 1)
    for t, (r, c) in enumerate(tiles):
        got = pieces_got[t // per, t % per].astype(f32)
        token = lax.broadcasted_iota(jnp.int32, (16, 128), 1) + c
        drop = jnp.where(token < CLIP, drop_clip, drop_t5)
        own = null_pad[r : r + 16, c : c + 128].astype(f32)
        at = pl.ds(pl.multiple_of(me * depth + r, 16), 16)
        rows_t[at, c : c + 128] = jnp.where(drop == 1, own, got).astype(bf16)

    def block(s):
        return rows_t.at[pl.ds(pl.multiple_of(s * depth, 16), depth)]

    def send_c(o):
        return remote(block(me), block(me), sems_c, (o,), (dp, me ^ o))

    def recv_c(o):
        return remote(block(me), block(me ^ o), sems_c, (o,), (dp, me ^ o))

    def send_f(o):
        return remote(block(me ^ o), block(me ^ o), sems_f, (o,), (dp, me ^ 1))

    def recv_f(o):
        return remote(block(me ^ 1), block(me ^ 1 ^ o), sems_f, (o,), (dp, me ^ 1))

    far = list(range(2, n_seq, 2))
    for o in far + [1]:
        send_c(o).start()
    for h in range(1, heads):
        each(n_seq, lambda o: send_in(h, o).start(), 1)
    for o in far:
        recv_c(o).wait_recv()
        send_f(o).start()
    recv_c(1).wait_recv()
    for o in far:
        recv_f(o).wait_recv()
    w_copy.wait()

    def send_out(h, o):
        return remote(
            out_all.at[h, peer_rows(o)], back.at[h, me], sems_out, (h, o), (dp, me ^ o)
        )

    def recv_out(h, o):
        return remote(
            out_all.at[h, mine_rows], back.at[h, me ^ o], sems_out, (h, o), (dp, me ^ o)
        )

    def ranges(g, side):
        lo, hi = GROUPS[g][side]
        return pl.ds(lo, hi - lo)

    def along(side, o):
        return (mx * ny + (my ^ o), me) if side == 0 else ((mx ^ o) * ny + my, me)

    def first(g, side, o, sending):
        here = my if side == 0 else mx
        other = here ^ o
        to = other if sending else here
        lane = ranges(g, side)
        src = term.at[:, to, :, lane] if side == 0 else term.at[to, :, :, lane]
        slot = here if sending else other
        return remote(
            src, term_in.at[side, slot, :, :, lane], sems_1, (g, side, o), along(side, o)
        )

    def second(g, side, o, sending):
        here = mx if side == 0 else my
        other = here ^ o
        lane = ranges(g, side)
        to = other if sending else here
        slot = here if sending else other
        return remote(
            part.at[to, :, lane],
            part_in.at[slot, :, lane],
            sems_2,
            (g, side, o),
            along(1 - side, o),
        )

    def sides_of(g):
        return [side for side in range(2) if GROUPS[g][side] is not None]

    def finish_heads(g):
        sides = sides_of(g)
        lo, hi = GROUPS[g][sides[0]][0], GROUPS[g][sides[-1]][1]
        a1, b1 = [out_all[g, img:nk, c : c + 128] for c in (0, 128)]
        low = low_lanes(a1.shape)
        if g % 2:
            b0 = out_all[g - 1, img:nk, 128:256]
            d_text[:, lo : lo + 128] = jnp.where(low, swap_halves(b0), swap_halves(a1))
            d_text[:, lo + 128 : lo + 256] = b1
        else:
            rb = swap_halves(b1)
            d_text[:, lo : lo + 128] = jnp.where(low, a1, rb)
            if hi - lo > 128:
                d_text[:, lo + 128 : hi] = jnp.where(low, rb, jnp.zeros_like(rb))
        run = 4 * chunk_rows

        def multiply(x):
            a = rows_t[pl.ds(pl.multiple_of(x * run, 16), run), 0:txt_pad]
            d = dot(a, d_text[:, lo:hi])
            pad = jnp.zeros((term.shape[2] - chunk_rows, hi - lo), f32)
            for j in range(4):
                v = jnp.concatenate([d[j * chunk_rows : (j + 1) * chunk_rows], pad], 0)
                i = 4 * x + j
                term[i // ny, i % ny, :, lo:hi] = v.astype(bf16)

        each(nx * ny // 4, multiply)
        for side in sides_of(g):
            for o in range(1, ny if side == 0 else nx):
                first(g, side, o, True).start()

    def add_first(g):
        for side in sides_of(g):
            k = ny if side == 0 else nx
            for o in range(1, k):
                first(g, side, o, False).wait_recv()
            here = my if side == 0 else mx
            lane = ranges(g, side)

            def add(j):
                own = term[j, here, :, lane] if side == 0 else term[here, j, :, lane]
                total = own.astype(f32)
                for o in range(1, k):
                    total = total + term_in[side, here ^ o, j, :, lane].astype(f32)
                part[j, :, lane] = total.astype(bf16)

            n = nx if side == 0 else ny
            each(n, add)
            for o in range(1, n):
                second(g, side, o, True).start()

    def add_second(g):
        for side in sides_of(g):
            n = nx if side == 0 else ny
            for o in range(1, n):
                second(g, side, o, False).wait_recv()
            here = mx if side == 0 else my
            lane = ranges(g, side)
            total = part[here, :, lane].astype(f32)
            for o in range(1, n):
                total = total + part_in[here ^ o, :, lane].astype(f32)
            size = min(lane.start + lane.size, d_w.shape[1]) - lane.start
            d_w[:, lane.start : lane.start + size] = total[0:chunk_rows, 0:size]

    def one_head(h):
        wide = 3 * HD
        w_rows = pl.ds(pl.multiple_of(h * wide, HD), wide)
        xt[0:wide, img:n_x] = dot(w_t[w_rows, :], rows_t[...]).astype(bf16)
        head_rows = pl.ds(pl.multiple_of(h * HD, HD), HD)
        xt[wide:256, img:n_x] = text_cot[head_rows, :]
        x, out = x_all.at[h], out_all.at[h]
        x[img:n_x, :] = xt[:, img:n_x].T
        acc[...] = jnp.zeros_like(acc)
        each(n_seq, lambda o: recv_in(h, o).wait_recv(), 1)
        for r in range(0, img, BQ):
            xt[:, r : r + BQ] = x[r : r + BQ, :].T
        all_blocks(
            nq // BQ, img, nk, x, xt, bias, s_scr, e_scrs, states, acc, out, attended_t
        )
        for k, n in chunks(nk, KC):
            out[k : k + n, 128:256] = acc[k : k + n, :].astype(bf16)
        each(n_seq, lambda o: send_out(h, o).start(), 1)
        back[h, me] = out[mine_rows, :]
        text_out[head_rows, :] = attended_t[:, img : img + txt]
        for g in range(len(GROUPS)):
            if g + 2 < len(GROUPS):
                pl.when(h == g + 2)(functools.partial(add_second, g))
            if g + 1 < len(GROUPS):
                pl.when(h == g + 1)(functools.partial(add_first, g))
        for g in range(len(GROUPS)):
            pl.when(h == g)(functools.partial(finish_heads, g))

    each(heads, one_head)

    add_second(len(GROUPS) - 2)
    add_first(len(GROUPS) - 1)
    for h in range(heads):
        each(n_seq, lambda o: recv_out(h, o).wait_recv(), 1)
    add_second(len(GROUPS) - 1)

    each(n_dp, lambda o: send_a(o).wait_send(), 1)
    each(n_dp, lambda o: send_b(o).wait_send(), 1)
    for o in far + [1]:
        send_c(o).wait_send()
    for o in far:
        send_f(o).wait_send()
    for h in range(heads):
        each(n_seq, lambda o: send_in(h, o).wait_send(), 1)
        each(n_seq, lambda o: send_out(h, o).wait_send(), 1)
    for g in range(len(GROUPS)):
        for side in sides_of(g):
            for o in range(1, ny if side == 0 else nx):
                first(g, side, o, True).wait_send()
            for o in range(1, nx if side == 0 else ny):
                second(g, side, o, True).wait_send()


def unpack_kernel(back, text_in, d_w_in, img_out, text_out, d_qkv, d_w):
    heads, n_seq = back.shape[0], back.shape[1]
    for p in range(n_seq * heads // 2):
        v = []
        for j in range(2):
            s, h = divmod(2 * p + j, heads)
            v += [back[h, s, :, 0:128], back[h, s, :, 128:256]]
        t = join_pair(*v)
        for j in range(3):
            d_qkv[:, p * 384 + 128 * j : p * 384 + 128 * j + 128] = t[j]
        img_out[:, p * 128 : p * 128 + 128] = t[3]
    text_out[...] = text_in[...]
    d_w[...] = d_w_in[...]


def on_device(
    img_qkv,
    text_cache,
    null_rows,
    w_text,
    cache_owner,
    cache_row,
    dropped,
    text_length,
    d_img_out,
    d_text_out,
):
    n_dp, n_seq = lax.axis_size("dp"), lax.axis_size("seq")
    ny = 4
    nx = n_dp // ny
    txt, depth = null_rows.shape
    tokens = img_qkv.shape[1]
    width = w_text.shape[1]
    heads = width // (3 * HD)
    img = tokens * n_seq
    nk = -(-(img + txt) // 16) * 16
    nq = -(-(img + txt) // BQ) * BQ
    txt_pad = nk - img
    lanes = -(-txt // 128) * 128
    per = -(-(depth // 16 * (lanes // 128)) // n_dp)
    chunk_rows = depth * n_seq // n_dp
    chunk_pad = -(-chunk_rows // 16) * 16
    wide = -(-width // 128) * 128
    vmem = pl.BlockSpec(memory_space=pltpu.VMEM)
    smem = pl.BlockSpec(memory_space=pltpu.SMEM)
    dma = pltpu.SemaphoreType.DMA
    out_shape = (
        jax.ShapeDtypeStruct((heads, n_seq, tokens, 256), bf16),
        jax.ShapeDtypeStruct((heads * HD, txt), bf16),
        jax.ShapeDtypeStruct((chunk_rows, width), f32),
    )
    scratch = [
        pltpu.VMEM((n_seq, heads, tokens, 256), bf16),
        pltpu.VMEM((heads, img + lanes, 256), bf16),
        pltpu.VMEM((heads, nq, 256), bf16),
        pltpu.VMEM((HD, nq), bf16),
        pltpu.VMEM((width, n_seq * depth), bf16),
        pltpu.VMEM((n_seq * depth, lanes), bf16),
        pltpu.VMEM((heads * HD, lanes), bf16),
        pltpu.VMEM((depth, lanes), bf16),
        pltpu.VMEM((depth, lanes), bf16),
        pltpu.VMEM((n_dp, per, 16, 128), bf16),
        pltpu.VMEM((n_dp, per, 16, 128), bf16),
        pltpu.VMEM((n_dp, per, 16, 128), bf16),
        pltpu.VMEM((n_dp, per, 16, 128), bf16),
        pltpu.VMEM((txt_pad, wide), bf16),
        pltpu.VMEM((nx, ny, chunk_pad, wide), bf16),
        pltpu.VMEM((2, ny, nx, chunk_pad, wide), bf16),
        pltpu.VMEM((nx, chunk_pad, wide), bf16),
        pltpu.VMEM((nx, chunk_pad, wide), bf16),
        pltpu.VMEM((txt_pad, 128), f32),
        pltpu.VMEM((256, nq), bf16),
        pltpu.VMEM((nk, BQ), f32),
        pltpu.VMEM((nk, BQ), bf16),
        pltpu.VMEM((nk, BQ), bf16),
        pltpu.VMEM((nk, 128), f32),
        pltpu.VMEM((128, BQ), bf16),
        pltpu.VMEM((128, BQ), bf16),
        pltpu.VMEM((BQ, 128), bf16),
        pltpu.VMEM((BQ, 128), bf16),
        pltpu.VMEM((BQ, 128), bf16),
        pltpu.VMEM((BQ, 128), bf16),
        pltpu.VMEM((8, BQ), f32),
        pltpu.VMEM((8, BQ), f32),
        pltpu.VMEM((HD, BQ), bf16),
        pltpu.VMEM((HD, BQ), bf16),
        dma,
        dma((2, n_dp)),
        dma((2, n_dp)),
        dma((2, n_seq)),
        dma((2, n_seq)),
        dma((2, heads, n_seq)),
        dma((2, heads, n_seq)),
        dma((2, len(GROUPS), 2, max(nx, ny))),
        dma((2, len(GROUPS), 2, max(nx, ny))),
    ]
    back, text_out, d_w = pl.pallas_call(
        functools.partial(kernel, (n_dp, n_seq, nx, ny)),
        out_shape=out_shape,
        in_specs=[vmem, vmem, vmem, vmem, pl.BlockSpec(memory_space=pl.ANY)]
        + [smem] * 4
        + [vmem],
        out_specs=(vmem,) * 3,
        scratch_shapes=scratch,
        compiler_params=pltpu.CompilerParams(
            collective_id=0, has_side_effects=True, vmem_limit_bytes=62 * 2**20
        ),
    )(
        img_qkv[0],
        d_img_out[0],
        text_cache.transpose(0, 2, 1),
        null_rows.T,
        w_text.T,
        cache_owner,
        cache_row,
        dropped.T,
        text_length,
        d_text_out[0].T,
    )
    steps = 4
    part = tokens // steps
    whole = [pl.BlockSpec(a.shape, lambda i: (0, 0)) for a in (text_out, d_w)]
    img_out, text_out, d_qkv, d_w = pl.pallas_call(
        unpack_kernel,
        grid=(steps,),
        out_shape=(
            jax.ShapeDtypeStruct((tokens, n_seq * heads * HD), bf16),
            jax.ShapeDtypeStruct(text_out.shape, bf16),
            jax.ShapeDtypeStruct((tokens, n_seq * width), bf16),
            jax.ShapeDtypeStruct(d_w.shape, f32),
        ),
        in_specs=[pl.BlockSpec((heads, n_seq, part, 256), lambda i: (0, 0, i, 0))] + whole,
        out_specs=(
            pl.BlockSpec((part, n_seq * heads * HD), lambda i: (i, 0)),
            whole[0],
            pl.BlockSpec((part, n_seq * width), lambda i: (i, 0)),
            whole[1],
        ),
        compiler_params=pltpu.CompilerParams(vmem_limit_bytes=32 * 2**20),
    )(back, text_out, d_w)
    return (img_out[None], text_out.T[None], d_qkv[None], d_w)


def solution(mesh):
    return jax.shard_map(
        on_device,
        mesh=mesh,
        in_specs=(
            P("dp", "seq", None),
            P("dp", None, "seq"),
            P(None, "seq"),
            P(None, "seq"),
            P(),
            P(),
            P(),
            P(),
            P("dp", "seq", None),
            P("dp", None, "seq"),
        ),
        out_specs=(
            P("dp", "seq", None),
            P("dp", None, "seq"),
            P("dp", "seq", None),
            P("dp", "seq"),
        ),
        check_vma=False,
    )
```

```python
import functools

import jax
import jax.numpy as jnp
from jax import lax
from jax.experimental import pallas as pl
from jax.experimental.pallas import tpu as pltpu
from jax.sharding import PartitionSpec as P

HD = 64
CLIP = 77
BQ = 256
KC = 464
f32, bf16 = jnp.float32, jnp.bfloat16


def chunks(n, c):
    return [(s, min(c, n - s)) for s in range(0, n, c)]


def dot(a, b):
    return jnp.dot(a, b, preferred_element_type=f32)


def fold(x, op):
    parts = [x[8 * i : 8 * i + 8] for i in range(x.shape[0] // 8)]
    while len(parts) > 1:
        parts = [
            op(parts[j], parts[j + 1]) if j + 1 < len(parts) else parts[j]
            for j in range(0, len(parts), 2)
        ]
    return parts[0]


def forward_block(i, img, nk, x, xt, bias, s_scr, e_scr, state, wq=BQ):
    w_probs, w_values, w_keys, delta, attended = state
    q0 = pl.multiple_of(i * BQ, BQ)
    zeros = jnp.zeros((HD, wq), bf16)
    q_t = xt[0:64, pl.ds(q0, wq)] * bf16(0.125)
    w_scores = jnp.concatenate([zeros, q_t], 0)
    top8 = None
    for k, n in chunks(nk, KC):
        s = dot(x[k : k + n, 0:128], w_scores)
        if k + n > img:
            b = bias[max(k - img, 0) : k + n - img, :]
            b = jnp.concatenate([b] * (wq // 128), 1)
            s = s + b if k >= img else jnp.concatenate([s[: img - k], s[img - k :] + b], 0)
        s_scr[k : k + n, 0:wq] = s
        c = fold(s, jnp.maximum)
        top8 = c if top8 is None else jnp.maximum(top8, c)
        yield
    top = jnp.max(top8, 0, keepdims=True)
    sum8 = out_t = None
    for k, n in chunks(nk, KC):
        e = jnp.exp(s_scr[k : k + n, 0:wq] - top)
        c = fold(e, jnp.add)
        sum8 = c if sum8 is None else sum8 + c
        e = e.astype(bf16)
        e_scr[k : k + n, 0:wq] = e
        o = dot(xt[128:192, k : k + n], e)
        out_t = o if out_t is None else out_t + o
        yield
    cot_t = xt[192:256, pl.ds(q0, wq)].astype(f32)
    inv = 1.0 / jnp.sum(sum8, 0, keepdims=True)
    out_t = (out_t * inv).astype(bf16)
    row_delta = jnp.sum(cot_t * out_t.astype(f32), 0, keepdims=True) * inv
    cot_s = (cot_t * inv).astype(bf16)
    w_probs[:, 0:wq] = jnp.concatenate([cot_s, zeros], 0)
    w_values[0:wq, :] = jnp.concatenate([zeros, cot_s], 0).T
    w_keys[0:wq, :] = jnp.concatenate([q_t, zeros], 0).T
    delta[:, 0:wq] = jnp.broadcast_to(row_delta, (delta.shape[0], wq))
    attended[:, 0:wq] = out_t


def backward_block(i, nk, x, xt, e_scr, state, acc, out, attended_t, wq=BQ):
    w_probs, w_values, w_keys, delta, attended = state
    q0 = pl.multiple_of(i * BQ, BQ)
    row_delta = delta[0:1, 0:wq]
    dq_t = None
    for k, n in chunks(nk, KC):
        dp = dot(x[k : k + n, 128:256], w_probs[:, 0:wq])
        e = e_scr[k : k + n, 0:wq]
        ds = (e.astype(f32) * (dp - row_delta)).astype(bf16)
        d = dot(xt[64:128, k : k + n], ds)
        dq_t = d if dq_t is None else dq_t + d
        acc[k : k + n, :] += dot(ds, w_keys[0:wq, :]) + dot(e, w_values[0:wq, :])
        yield
    dq_t = (dq_t * 0.125).astype(bf16)
    out[pl.ds(q0, wq), 0:128] = jnp.concatenate([dq_t, attended[:, 0:wq]], 0).T
    attended_t[:, pl.ds(q0, wq)] = attended[:, 0:wq]


def alternate(a, b):
    live = [True, True]
    turn = 0
    while live[0] or live[1]:
        g = 1 if turn % 3 == 2 else 0
        turn += 1
        if live[g]:
            live[g] = next((a, b)[g], "end") is None


def all_blocks(n, img, nk, x, xt, bias, s_scr, e_scrs, states, acc, out, attended_t):
    last = -(-(nk - (n - 1) * BQ) // 128) * 128

    def forward(i, side, wq=BQ):
        return forward_block(i, img, nk, x, xt, bias, s_scr, e_scrs[side], states[side], wq)

    def backward(i, side, wq=BQ):
        return backward_block(
            i, nk, x, xt, e_scrs[side], states[side], acc, out, attended_t, wq
        )

    for _ in forward(0, 0):
        pass

    def body(j, c):
        alternate(forward(2 * j + 1, 1), backward(2 * j, 0))
        alternate(forward(2 * j + 2, 0), backward(2 * j + 1, 1))
        return c

    lax.fori_loop(0, n // 2 - 1, body, 0)
    alternate(forward(n - 1, 1, last), backward(n - 2, 0))
    for _ in backward(n - 1, 1, last):
        pass


def swap_halves(v):
    return jnp.concatenate([v[:, HD:], v[:, :HD]], 1)


def low_lanes(shape):
    return lax.broadcasted_iota(jnp.int32, shape, 1) < HD


def split_pair(t0, t1, t2, cot):
    low = low_lanes(t0.shape)
    r1, r2, rc = swap_halves(t1), swap_halves(t2), swap_halves(cot)
    return (t0, jnp.where(low, t1, rc)), (jnp.where(low, r1, r2), jnp.where(low, r2, cot))


def join_pair(a0, b0, a1, b1):
    low = low_lanes(a0.shape)
    ra0, rb0, ra1 = swap_halves(a0), swap_halves(b0), swap_halves(a1)
    return (
        jnp.where(low, a0, rb0),
        jnp.where(low, rb0, ra1),
        b1,
        jnp.where(low, ra0, a1),
    )


def tiles_of(rows, lanes):
    return [(r, c) for r in range(0, rows, 16) for c in range(0, lanes, 128)]


GROUPS = (
    ((0, 128), None),
    ((128, 256), (256, 384)),
    (None, (384, 512)),
    ((512, 640), (640, 768)),
    ((768, 896), (896, 1024)),
)


def kernel(
    dims,
    qkv,
    cot_img,
    cache,
    null_rows,
    w_hbm,
    owner,
    cache_row,
    dropped,
    length,
    cot_text,
    back,
    text_out,
    d_w,
    packed,
    x_all,
    out_all,
    attended_t,
    w_t,
    rows_t,
    text_qkv,
    text_cot,
    raw,
    null_pad,
    pieces,
    pieces_in,
    pieces_out,
    pieces_got,
    d_text,
    term,
    term_in,
    part,
    part_in,
    bias,
    xt,
    s_scr,
    e_scr0,
    e_scr1,
    acc,
    st_a0,
    st_a1,
    st_b0,
    st_b1,
    st_c0,
    st_c1,
    st_d0,
    st_d1,
    st_e0,
    st_e1,
    sem_w,
    sems_a,
    sems_b,
    sems_c,
    sems_f,
    sems_in,
    sems_out,
    sems_1,
    sems_2,
):
    n_dp, n_seq, nx, ny = dims
    dp, me = lax.axis_index("dp"), lax.axis_index("seq")
    mx, my = dp // ny, dp % ny
    tokens = qkv.shape[0]
    heads = x_all.shape[0]
    nq = xt.shape[1]
    n_x = x_all.shape[1]
    img = tokens * n_seq
    nk = e_scr0.shape[0]
    e_scrs = (e_scr0, e_scr1)
    states = ((st_a0, st_b0, st_c0, st_d0, st_e0), (st_a1, st_b1, st_c1, st_d1, st_e1))
    txt_pad = nk - img
    depth, txt = null_rows.shape
    lanes = raw.shape[1]
    per = pieces.shape[1]
    chunk_rows = d_w.shape[0]

    def remote(src, dst, sems, at, dev):
        return pltpu.make_async_remote_copy(
            src_ref=src,
            dst_ref=dst,
            send_sem=sems.at[(0,) + at],
            recv_sem=sems.at[(1,) + at],
            device_id=dev,
            device_id_type=pl.DeviceIdType.MESH,
        )

    def each(n, fn, start=0):
        def body(i, c):
            fn(i)
            return c

        lax.fori_loop(start, n, body, 0)

    barrier = pltpu.get_barrier_semaphore()

    def greet_seq(o):
        pl.semaphore_signal(
            barrier, inc=1, device_id=(dp, me ^ o), device_id_type=pl.DeviceIdType.MESH
        )

    def greet_dp(o):
        pl.semaphore_signal(
            barrier, inc=1, device_id=(dp ^ o, me), device_id_type=pl.DeviceIdType.MESH
        )

    each(n_seq, greet_seq, 1)
    each(n_dp, greet_dp, 1)
    w_copy = pltpu.make_async_copy(w_hbm, w_t, sem_w)
    w_copy.start()

    mine = jnp.int32(0)
    for b in range(n_dp):
        mine = jnp.where(owner[b] == dp, jnp.int32(b), mine)
    row = cache_row[mine]
    raw[...] = jnp.zeros_like(raw)
    raw[:, 0:txt] = cache[row]
    null_pad[...] = jnp.zeros_like(null_pad)
    null_pad[:, 0:txt] = null_rows[...]
    tiles = tiles_of(depth, lanes)
    for t, (r, c) in enumerate(tiles):
        pieces[t // per, t % per] = raw[r : r + 16, c : c + 128]
    for t in range(len(tiles), n_dp * per):
        pieces[t // per, t % per] = jnp.zeros((16, 128), bf16)
    pieces_in[dp] = pieces[dp]

    def pack(p):
        c = pl.multiple_of(p * 384, 128)
        t = [qkv[:, pl.ds(pl.multiple_of(c + 128 * j, 128), 128)] for j in range(3)]
        g = cot_img[:, pl.ds(pl.multiple_of(p * 128, 128), 128)]
        for j, (a, b) in enumerate(split_pair(*t, g)):
            head = 2 * p + j
            to, h = head // heads, head % heads
            packed[to, h, :, 0:128] = a
            packed[to, h, :, 128:256] = b

    lax.fori_loop(0, n_seq, lambda i, c: (pack(i * heads // 2), c)[1], 0, unroll=2)

    pl.semaphore_wait(barrier, n_seq + n_dp - 2)

    def send_a(o):
        return remote(pieces.at[dp ^ o], pieces_in.at[dp], sems_a, (o,), (dp ^ o, me))

    def recv_a(o):
        return remote(pieces.at[dp], pieces_in.at[dp ^ o], sems_a, (o,), (dp ^ o, me))

    each(n_dp, lambda o: send_a(o).start(), 1)

    mine_rows = pl.ds(pl.multiple_of(me * tokens, tokens), tokens)

    def peer_rows(o):
        return pl.ds(pl.multiple_of((me ^ o) * tokens, tokens), tokens)

    def send_in(h, o):
        return remote(
            packed.at[me ^ o, h], x_all.at[h, mine_rows], sems_in, (h, o), (dp, me ^ o)
        )

    def recv_in(h, o):
        return remote(
            packed.at[me, h], x_all.at[h, peer_rows(o)], sems_in, (h, o), (dp, me ^ o)
        )

    each(n_seq, lambda o: send_in(0, o).start(), 1)

    each(n_dp, lambda o: recv_a(o).wait_recv(), 1)
    for b in range(n_dp):
        pieces_out[b] = pieces_in[owner[b]]

    def send_b(o):
        return remote(pieces_out.at[dp ^ o], pieces_got.at[dp], sems_b, (o,), (dp ^ o, me))

    def recv_b(o):
        return remote(pieces_out.at[dp], pieces_got.at[dp ^ o], sems_b, (o,), (dp ^ o, me))

    each(n_dp, lambda o: send_b(o).start(), 1)
    pieces_got[dp] = pieces_out[dp]

    text_cot[...] = jnp.zeros_like(text_cot)
    text_cot[:, 0:txt] = cot_text[...]
    if nq > n_x:
        xt[:, n_x:nq] = jnp.zeros((256, nq - n_x), bf16)
    seen = lax.broadcasted_iota(jnp.int32, bias.shape, 0) < length[dp]
    bias[...] = jnp.where(seen, 0.0, -1e30)
    drop_clip, drop_t5 = dropped[0, dp], dropped[1, dp]

    each(n_dp, lambda o: recv_b(o).wait_recv(), 1)
    for t, (r, c) in enumerate(tiles):
        got = pieces_got[t // per, t % per].astype(f32)
        token = lax.broadcasted_iota(jnp.int32, (16, 128), 1) + c
        drop = jnp.where(token < CLIP, drop_clip, drop_t5)
        own = null_pad[r : r + 16, c : c + 128].astype(f32)
        at = pl.ds(pl.multiple_of(me * depth + r, 16), 16)
        rows_t[at, c : c + 128] = jnp.where(drop == 1, own, got).astype(bf16)

    def block(s):
        return rows_t.at[pl.ds(pl.multiple_of(s * depth, 16), depth)]

    def send_c(o):
        return remote(block(me), block(me), sems_c, (o,), (dp, me ^ o))

    def recv_c(o):
        return remote(block(me), block(me ^ o), sems_c, (o,), (dp, me ^ o))

    def send_f(o):
        return remote(block(me ^ o), block(me ^ o), sems_f, (o,), (dp, me ^ 1))

    def recv_f(o):
        return remote(block(me ^ 1), block(me ^ 1 ^ o), sems_f, (o,), (dp, me ^ 1))

    far = sorted(range(2, n_seq, 2), key=lambda o: o == n_seq // 2)
    for o in far[::-1] + [1]:
        send_c(o).start()
    def pack_rest(i):
        for j in (1, 3, 4):
            pack(i * heads + j)

    each(n_seq // 2, pack_rest)
    for h in range(1, heads):
        each(n_seq, lambda o: send_in(h, o).start(), 1)

    def own_image(h):
        x_all[h, mine_rows, :] = packed[me, h]

    each(heads, own_image)
    for o in far:
        recv_c(o).wait_recv()
        send_f(o).start()
    recv_c(1).wait_recv()
    for o in far:
        recv_f(o).wait_recv()
    w_copy.wait()
    half = w_t.shape[0] // 2
    for r in range(0, w_t.shape[0], half):
        text_qkv[r : r + half, :] = dot(w_t[r : r + half, :], rows_t[...]).astype(bf16)

    def send_out(h, o):
        return remote(
            out_all.at[h, peer_rows(o)], back.at[h, me], sems_out, (h, o), (dp, me ^ o)
        )

    def recv_out(h, o):
        return remote(
            out_all.at[h, mine_rows], back.at[h, me ^ o], sems_out, (h, o), (dp, me ^ o)
        )

    def ranges(g, side):
        lo, hi = GROUPS[g][side]
        return pl.ds(lo, hi - lo)

    def along(side, o):
        return (mx * ny + (my ^ o), me) if side == 0 else ((mx ^ o) * ny + my, me)

    def first(g, side, o, sending):
        here = my if side == 0 else mx
        other = here ^ o
        to = other if sending else here
        lane = ranges(g, side)
        src = term.at[:, to, :, lane] if side == 0 else term.at[to, :, :, lane]
        slot = here if sending else other
        return remote(
            src, term_in.at[side, slot, :, :, lane], sems_1, (g, side, o), along(side, o)
        )

    def second(g, side, o, sending):
        here = mx if side == 0 else my
        other = here ^ o
        lane = ranges(g, side)
        to = other if sending else here
        slot = here if sending else other
        return remote(
            part.at[to, :, lane],
            part_in.at[slot, :, lane],
            sems_2,
            (g, side, o),
            along(1 - side, o),
        )

    def sides_of(g):
        return [side for side in range(2) if GROUPS[g][side] is not None]

    def finish_heads(g):
        sides = sides_of(g)
        lo, hi = GROUPS[g][sides[0]][0], GROUPS[g][sides[-1]][1]
        a1, b1 = [out_all[g, img:nk, c : c + 128] for c in (0, 128)]
        low = low_lanes(a1.shape)
        if g % 2:
            b0 = out_all[g - 1, img:nk, 128:256]
            d_text[:, lo : lo + 128] = jnp.where(low, swap_halves(b0), swap_halves(a1))
            d_text[:, lo + 128 : lo + 256] = b1
        else:
            rb = swap_halves(b1)
            d_text[:, lo : lo + 128] = jnp.where(low, a1, rb)
            if hi - lo > 128:
                d_text[:, lo + 128 : hi] = jnp.where(low, rb, jnp.zeros_like(rb))
        run = 4 * chunk_rows

        def multiply(x):
            a = rows_t[pl.ds(pl.multiple_of(x * run, 16), run), 0:txt_pad]
            d = dot(a, d_text[:, lo:hi])
            pad = jnp.zeros((term.shape[2] - chunk_rows, hi - lo), f32)
            for j in range(4):
                v = jnp.concatenate([d[j * chunk_rows : (j + 1) * chunk_rows], pad], 0)
                i = 4 * x + j
                term[i // ny, i % ny, :, lo:hi] = v.astype(bf16)

        each(nx * ny // 4, multiply)
        for side in sides_of(g):
            for o in range(1, ny if side == 0 else nx):
                first(g, side, o, True).start()

    def add_first(g):
        for side in sides_of(g):
            k = ny if side == 0 else nx
            for o in range(1, k):
                first(g, side, o, False).wait_recv()
            here = my if side == 0 else mx
            lane = ranges(g, side)

            def add(j):
                own = term[j, here, :, lane] if side == 0 else term[here, j, :, lane]
                total = own.astype(f32)
                for o in range(1, k):
                    total = total + term_in[side, here ^ o, j, :, lane].astype(f32)
                part[j, :, lane] = total.astype(bf16)

            n = nx if side == 0 else ny
            each(n, add)
            for o in range(1, n):
                second(g, side, o, True).start()

    def add_second(g):
        for side in sides_of(g):
            n = nx if side == 0 else ny
            for o in range(1, n):
                second(g, side, o, False).wait_recv()
            here = mx if side == 0 else my
            lane = ranges(g, side)
            total = part[here, :, lane].astype(f32)
            for o in range(1, n):
                total = total + part_in[here ^ o, :, lane].astype(f32)
            size = min(lane.start + lane.size, d_w.shape[1]) - lane.start
            d_w[:, lane.start : lane.start + size] = total[0:chunk_rows, 0:size]

    def one_head(h):
        wide = 3 * HD
        w_rows = pl.ds(pl.multiple_of(h * wide, HD), wide)
        xt[0:wide, img:n_x] = text_qkv[w_rows, :]
        head_rows = pl.ds(pl.multiple_of(h * HD, HD), HD)
        xt[wide:256, img:n_x] = text_cot[head_rows, :]
        x, out = x_all.at[h], out_all.at[h]
        x[img:n_x, :] = xt[:, img:n_x].T
        acc[...] = jnp.zeros_like(acc)
        each(n_seq, lambda o: recv_in(h, o).wait_recv(), 1)
        for r in range(0, img, BQ):
            xt[:, r : r + BQ] = x[r : r + BQ, :].T
        all_blocks(
            nq // BQ, img, nk, x, xt, bias, s_scr, e_scrs, states, acc, out, attended_t
        )
        for k, n in chunks(nk, KC):
            out[k : k + n, 128:256] = acc[k : k + n, :].astype(bf16)
        each(n_seq, lambda o: send_out(h, o).start(), 1)
        back[h, me] = out[mine_rows, :]
        text_out[head_rows, :] = attended_t[:, img : img + txt]
        for g in range(len(GROUPS)):
            pl.when(h == g)(functools.partial(finish_heads, g))
        for g in range(len(GROUPS)):
            if g + 2 < len(GROUPS):
                pl.when(h == g + 2)(functools.partial(add_second, g))
            if g + 1 < len(GROUPS):
                pl.when(h == g + 1)(functools.partial(add_first, g))

    each(heads, one_head)

    add_second(len(GROUPS) - 2)
    add_first(len(GROUPS) - 1)
    for h in range(heads):
        each(n_seq, lambda o: recv_out(h, o).wait_recv(), 1)
    add_second(len(GROUPS) - 1)

    each(n_dp, lambda o: send_a(o).wait_send(), 1)
    each(n_dp, lambda o: send_b(o).wait_send(), 1)
    for o in far + [1]:
        send_c(o).wait_send()
    for o in far:
        send_f(o).wait_send()
    for h in range(heads):
        each(n_seq, lambda o: send_in(h, o).wait_send(), 1)
        each(n_seq, lambda o: send_out(h, o).wait_send(), 1)
    for g in range(len(GROUPS)):
        for side in sides_of(g):
            for o in range(1, ny if side == 0 else nx):
                first(g, side, o, True).wait_send()
            for o in range(1, nx if side == 0 else ny):
                second(g, side, o, True).wait_send()


def unpack_kernel(back, text_in, d_w_in, img_out, text_out, d_qkv, d_w):
    heads, n_seq = back.shape[0], back.shape[1]
    for p in range(n_seq * heads // 2):
        v = []
        for j in range(2):
            s, h = divmod(2 * p + j, heads)
            v += [back[h, s, :, 0:128], back[h, s, :, 128:256]]
        t = join_pair(*v)
        for j in range(3):
            d_qkv[:, p * 384 + 128 * j : p * 384 + 128 * j + 128] = t[j]
        img_out[:, p * 128 : p * 128 + 128] = t[3]
    text_out[...] = text_in[...]
    d_w[...] = d_w_in[...]


def on_device(
    img_qkv,
    text_cache,
    null_rows,
    w_text,
    cache_owner,
    cache_row,
    dropped,
    text_length,
    d_img_out,
    d_text_out,
):
    n_dp, n_seq = lax.axis_size("dp"), lax.axis_size("seq")
    ny = 4
    nx = n_dp // ny
    txt, depth = null_rows.shape
    tokens = img_qkv.shape[1]
    width = w_text.shape[1]
    heads = width // (3 * HD)
    img = tokens * n_seq
    nk = -(-(img + txt) // 16) * 16
    nq = -(-(img + txt) // BQ) * BQ
    txt_pad = nk - img
    lanes = -(-txt // 128) * 128
    per = -(-(depth // 16 * (lanes // 128)) // n_dp)
    chunk_rows = depth * n_seq // n_dp
    chunk_pad = -(-chunk_rows // 16) * 16
    wide = -(-width // 128) * 128
    vmem = pl.BlockSpec(memory_space=pltpu.VMEM)
    smem = pl.BlockSpec(memory_space=pltpu.SMEM)
    dma = pltpu.SemaphoreType.DMA
    out_shape = (
        jax.ShapeDtypeStruct((heads, n_seq, tokens, 256), bf16),
        jax.ShapeDtypeStruct((heads * HD, txt), bf16),
        jax.ShapeDtypeStruct((chunk_rows, width), f32),
    )
    scratch = [
        pltpu.VMEM((n_seq, heads, tokens, 256), bf16),
        pltpu.VMEM((heads, img + lanes, 256), bf16),
        pltpu.VMEM((heads, nq, 256), bf16),
        pltpu.VMEM((HD, nq), bf16),
        pltpu.VMEM((width, n_seq * depth), bf16),
        pltpu.VMEM((n_seq * depth, lanes), bf16),
        pltpu.VMEM((width, lanes), bf16),
        pltpu.VMEM((heads * HD, lanes), bf16),
        pltpu.VMEM((depth, lanes), bf16),
        pltpu.VMEM((depth, lanes), bf16),
        pltpu.VMEM((n_dp, per, 16, 128), bf16),
        pltpu.VMEM((n_dp, per, 16, 128), bf16),
        pltpu.VMEM((n_dp, per, 16, 128), bf16),
        pltpu.VMEM((n_dp, per, 16, 128), bf16),
        pltpu.VMEM((txt_pad, wide), bf16),
        pltpu.VMEM((nx, ny, chunk_pad, wide), bf16),
        pltpu.VMEM((2, ny, nx, chunk_pad, wide), bf16),
        pltpu.VMEM((nx, chunk_pad, wide), bf16),
        pltpu.VMEM((nx, chunk_pad, wide), bf16),
        pltpu.VMEM((txt_pad, 128), f32),
        pltpu.VMEM((256, nq), bf16),
        pltpu.VMEM((nk, BQ), f32),
        pltpu.VMEM((nk, BQ), bf16),
        pltpu.VMEM((nk, BQ), bf16),
        pltpu.VMEM((nk, 128), f32),
        pltpu.VMEM((128, BQ), bf16),
        pltpu.VMEM((128, BQ), bf16),
        pltpu.VMEM((BQ, 128), bf16),
        pltpu.VMEM((BQ, 128), bf16),
        pltpu.VMEM((BQ, 128), bf16),
        pltpu.VMEM((BQ, 128), bf16),
        pltpu.VMEM((8, BQ), f32),
        pltpu.VMEM((8, BQ), f32),
        pltpu.VMEM((HD, BQ), bf16),
        pltpu.VMEM((HD, BQ), bf16),
        dma,
        dma((2, n_dp)),
        dma((2, n_dp)),
        dma((2, n_seq)),
        dma((2, n_seq)),
        dma((2, heads, n_seq)),
        dma((2, heads, n_seq)),
        dma((2, len(GROUPS), 2, max(nx, ny))),
        dma((2, len(GROUPS), 2, max(nx, ny))),
    ]
    back, text_out, d_w = pl.pallas_call(
        functools.partial(kernel, (n_dp, n_seq, nx, ny)),
        out_shape=out_shape,
        in_specs=[vmem, vmem, vmem, vmem, pl.BlockSpec(memory_space=pl.ANY)]
        + [smem] * 4
        + [vmem],
        out_specs=(vmem,) * 3,
        scratch_shapes=scratch,
        compiler_params=pltpu.CompilerParams(
            collective_id=0, has_side_effects=True, vmem_limit_bytes=62 * 2**20
        ),
    )(
        img_qkv[0],
        d_img_out[0],
        text_cache.transpose(0, 2, 1),
        null_rows.T,
        w_text.T,
        cache_owner,
        cache_row,
        dropped.T,
        text_length,
        d_text_out[0].T,
    )
    steps = 4
    part = tokens // steps
    whole = [pl.BlockSpec(a.shape, lambda i: (0, 0)) for a in (text_out, d_w)]
    img_out, text_out, d_qkv, d_w = pl.pallas_call(
        unpack_kernel,
        grid=(steps,),
        out_shape=(
            jax.ShapeDtypeStruct((tokens, n_seq * heads * HD), bf16),
            jax.ShapeDtypeStruct(text_out.shape, bf16),
            jax.ShapeDtypeStruct((tokens, n_seq * width), bf16),
            jax.ShapeDtypeStruct(d_w.shape, f32),
        ),
        in_specs=[pl.BlockSpec((heads, n_seq, part, 256), lambda i: (0, 0, i, 0))] + whole,
        out_specs=(
            pl.BlockSpec((part, n_seq * heads * HD), lambda i: (i, 0)),
            whole[0],
            pl.BlockSpec((part, n_seq * width), lambda i: (i, 0)),
            whole[1],
        ),
        compiler_params=pltpu.CompilerParams(vmem_limit_bytes=62 * 2**20),
    )(back, text_out, d_w)
    return (img_out[None], text_out.T[None], d_qkv[None], d_w)


def solution(mesh):
    return jax.shard_map(
        on_device,
        mesh=mesh,
        in_specs=(
            P("dp", "seq", None),
            P("dp", None, "seq"),
            P(None, "seq"),
            P(None, "seq"),
            P(),
            P(),
            P(),
            P(),
            P("dp", "seq", None),
            P("dp", None, "seq"),
        ),
        out_specs=(
            P("dp", "seq", None),
            P("dp", None, "seq"),
            P("dp", "seq", None),
            P("dp", "seq"),
        ),
        check_vma=False,
    )
```

```python
import functools

import jax
import jax.numpy as jnp
from jax import lax
from jax.experimental import pallas as pl
from jax.experimental.pallas import tpu as pltpu
from jax.sharding import PartitionSpec as P

HD = 64
CLIP = 77
BQ = 256
KC = 464
f32, bf16 = jnp.float32, jnp.bfloat16


def chunks(n, c):
    return [(s, min(c, n - s)) for s in range(0, n, c)]


def dot(a, b):
    return jnp.dot(a, b, preferred_element_type=f32)


def fold(x, op):
    parts = [x[8 * i : 8 * i + 8] for i in range(x.shape[0] // 8)]
    while len(parts) > 1:
        parts = [
            op(parts[j], parts[j + 1]) if j + 1 < len(parts) else parts[j]
            for j in range(0, len(parts), 2)
        ]
    return parts[0]


def forward_block(i, img, nk, x, xt, bias, s_scr, e_scr, state, wq=BQ):
    w_probs, w_values, w_keys, delta, attended = state
    q0 = pl.multiple_of(i * BQ, BQ)
    zeros = jnp.zeros((HD, wq), bf16)
    q_t = xt[0:64, pl.ds(q0, wq)] * bf16(0.125)
    w_scores = jnp.concatenate([zeros, q_t], 0)
    top8 = None
    for k, n in chunks(nk, KC):
        s = dot(x[k : k + n, 0:128], w_scores)
        if k + n > img:
            b = bias[max(k - img, 0) : k + n - img, :]
            b = jnp.concatenate([b] * (wq // 128), 1)
            s = s + b if k >= img else jnp.concatenate([s[: img - k], s[img - k :] + b], 0)
        s_scr[k : k + n, 0:wq] = s
        c = fold(s, jnp.maximum)
        top8 = c if top8 is None else jnp.maximum(top8, c)
        yield
    top = jnp.max(top8, 0, keepdims=True)
    sum8 = out_t = None
    for k, n in chunks(nk, KC):
        e = jnp.exp(s_scr[k : k + n, 0:wq] - top)
        c = fold(e, jnp.add)
        sum8 = c if sum8 is None else sum8 + c
        e = e.astype(bf16)
        e_scr[k : k + n, 0:wq] = e
        o = dot(xt[128:192, k : k + n], e)
        out_t = o if out_t is None else out_t + o
        yield
    cot_t = xt[192:256, pl.ds(q0, wq)].astype(f32)
    inv = 1.0 / jnp.sum(sum8, 0, keepdims=True)
    out_t = (out_t * inv).astype(bf16)
    row_delta = jnp.sum(cot_t * out_t.astype(f32), 0, keepdims=True) * inv
    cot_s = (cot_t * inv).astype(bf16)
    w_probs[:, 0:wq] = jnp.concatenate([cot_s, zeros], 0)
    w_values[0:wq, :] = jnp.concatenate([zeros, cot_s], 0).T
    w_keys[0:wq, :] = jnp.concatenate([q_t, zeros], 0).T
    delta[:, 0:wq] = jnp.broadcast_to(row_delta, (delta.shape[0], wq))
    attended[:, 0:wq] = out_t


def backward_block(i, nk, x, xt, e_scr, state, acc, out, attended_t, wq=BQ):
    w_probs, w_values, w_keys, delta, attended = state
    q0 = pl.multiple_of(i * BQ, BQ)
    row_delta = delta[0:1, 0:wq]
    dq_t = None
    for k, n in chunks(nk, KC):
        dp = dot(x[k : k + n, 128:256], w_probs[:, 0:wq])
        e = e_scr[k : k + n, 0:wq]
        ds = (e.astype(f32) * (dp - row_delta)).astype(bf16)
        d = dot(xt[64:128, k : k + n], ds)
        dq_t = d if dq_t is None else dq_t + d
        acc[k : k + n, :] += dot(ds, w_keys[0:wq, :]) + dot(e, w_values[0:wq, :])
        yield
    dq_t = (dq_t * 0.125).astype(bf16)
    out[pl.ds(q0, wq), 0:128] = jnp.concatenate([dq_t, attended[:, 0:wq]], 0).T
    attended_t[:, pl.ds(q0, wq)] = attended[:, 0:wq]


def alternate(a, b):
    live = [True, True]
    turn = 0
    while live[0] or live[1]:
        g = 1 if turn % 3 == 2 else 0
        turn += 1
        if live[g]:
            live[g] = next((a, b)[g], "end") is None


def all_blocks(n, img, nk, x, xt, bias, s_scr, e_scrs, states, acc, out, attended_t):
    last = -(-(nk - (n - 1) * BQ) // 128) * 128

    def forward(i, side, wq=BQ):
        return forward_block(i, img, nk, x, xt, bias, s_scr, e_scrs[side], states[side], wq)

    def backward(i, side, wq=BQ):
        return backward_block(
            i, nk, x, xt, e_scrs[side], states[side], acc, out, attended_t, wq
        )

    for _ in forward(0, 0):
        pass

    def body(j, c):
        alternate(forward(2 * j + 1, 1), backward(2 * j, 0))
        alternate(forward(2 * j + 2, 0), backward(2 * j + 1, 1))
        return c

    lax.fori_loop(0, n // 2 - 1, body, 0)
    alternate(forward(n - 1, 1, last), backward(n - 2, 0))
    for _ in backward(n - 1, 1, last):
        pass


def swap_halves(v):
    return jnp.concatenate([v[:, HD:], v[:, :HD]], 1)


def low_lanes(shape):
    return lax.broadcasted_iota(jnp.int32, shape, 1) < HD


def split_pair(t0, t1, t2, cot):
    low = low_lanes(t0.shape)
    r1, r2, rc = swap_halves(t1), swap_halves(t2), swap_halves(cot)
    return (t0, jnp.where(low, t1, rc)), (jnp.where(low, r1, r2), jnp.where(low, r2, cot))


def join_pair(a0, b0, a1, b1):
    low = low_lanes(a0.shape)
    ra0, rb0, ra1 = swap_halves(a0), swap_halves(b0), swap_halves(a1)
    return (
        jnp.where(low, a0, rb0),
        jnp.where(low, rb0, ra1),
        b1,
        jnp.where(low, ra0, a1),
    )


def tiles_of(rows, lanes):
    return [(r, c) for r in range(0, rows, 16) for c in range(0, lanes, 128)]


GROUPS = (
    ((0, 128), None),
    ((128, 256), (256, 384)),
    (None, (384, 512)),
    ((512, 640), (640, 768)),
    ((768, 896), (896, 1024)),
)


def kernel(
    dims,
    qkv,
    cot_img,
    cache,
    null_rows,
    w_hbm,
    owner,
    cache_row,
    dropped,
    length,
    cot_text,
    back,
    text_out,
    d_w,
    packed,
    x_all,
    out_all,
    attended_t,
    w_t,
    rows_t,
    text_qkv,
    text_cot,
    raw,
    null_pad,
    pieces,
    pieces_in,
    pieces_out,
    pieces_got,
    d_text,
    term,
    term_in,
    part,
    part_in,
    bias,
    xt,
    s_scr,
    e_scr0,
    e_scr1,
    acc,
    st_a0,
    st_a1,
    st_b0,
    st_b1,
    st_c0,
    st_c1,
    st_d0,
    st_d1,
    st_e0,
    st_e1,
    sem_w,
    sems_a,
    sems_b,
    sems_c,
    sems_f,
    sems_in,
    sems_out,
    sems_1,
    sems_2,
):
    n_dp, n_seq, nx, ny = dims
    dp, me = lax.axis_index("dp"), lax.axis_index("seq")
    mx, my = dp // ny, dp % ny
    tokens = qkv.shape[0]
    heads = x_all.shape[0]
    nq = xt.shape[1]
    n_x = x_all.shape[1]
    img = tokens * n_seq
    nk = e_scr0.shape[0]
    e_scrs = (e_scr0, e_scr1)
    states = ((st_a0, st_b0, st_c0, st_d0, st_e0), (st_a1, st_b1, st_c1, st_d1, st_e1))
    txt_pad = nk - img
    depth, txt = null_rows.shape
    lanes = raw.shape[1]
    per = pieces.shape[1]
    chunk_rows = d_w.shape[0]

    def remote(src, dst, sems, at, dev):
        return pltpu.make_async_remote_copy(
            src_ref=src,
            dst_ref=dst,
            send_sem=sems.at[(0,) + at],
            recv_sem=sems.at[(1,) + at],
            device_id=dev,
            device_id_type=pl.DeviceIdType.MESH,
        )

    def each(n, fn, start=0):
        def body(i, c):
            fn(i)
            return c

        lax.fori_loop(start, n, body, 0)

    barrier = pltpu.get_barrier_semaphore()

    def greet_seq(o):
        pl.semaphore_signal(
            barrier, inc=1, device_id=(dp, me ^ o), device_id_type=pl.DeviceIdType.MESH
        )

    def greet_dp(o):
        pl.semaphore_signal(
            barrier, inc=1, device_id=(dp ^ o, me), device_id_type=pl.DeviceIdType.MESH
        )

    each(n_seq, greet_seq, 1)
    each(n_dp, greet_dp, 1)
    w_copy = pltpu.make_async_copy(w_hbm, w_t, sem_w)
    w_copy.start()

    mine = jnp.int32(0)
    for b in range(n_dp):
        mine = jnp.where(owner[b] == dp, jnp.int32(b), mine)
    row = cache_row[mine]
    raw[...] = jnp.zeros_like(raw)
    raw[:, 0:txt] = cache[row]
    null_pad[...] = jnp.zeros_like(null_pad)
    null_pad[:, 0:txt] = null_rows[...]
    tiles = tiles_of(depth, lanes)
    for t, (r, c) in enumerate(tiles):
        pieces[t // per, t % per] = raw[r : r + 16, c : c + 128]
    for t in range(len(tiles), n_dp * per):
        pieces[t // per, t % per] = jnp.zeros((16, 128), bf16)
    pieces_in[dp] = pieces[dp]

    def pack(p):
        c = pl.multiple_of(p * 384, 128)
        t = [qkv[:, pl.ds(pl.multiple_of(c + 128 * j, 128), 128)] for j in range(3)]
        g = cot_img[:, pl.ds(pl.multiple_of(p * 128, 128), 128)]
        for j, (a, b) in enumerate(split_pair(*t, g)):
            head = 2 * p + j
            to, h = head // heads, head % heads
            packed[to, h, :, 0:128] = a
            packed[to, h, :, 128:256] = b

    lax.fori_loop(0, n_seq, lambda i, c: (pack(i * heads // 2), c)[1], 0, unroll=2)

    pl.semaphore_wait(barrier, n_seq + n_dp - 2)

    def send_a(o):
        return remote(pieces.at[dp ^ o], pieces_in.at[dp], sems_a, (o,), (dp ^ o, me))

    def recv_a(o):
        return remote(pieces.at[dp], pieces_in.at[dp ^ o], sems_a, (o,), (dp ^ o, me))

    each(n_dp, lambda o: send_a(o).start(), 1)

    mine_rows = pl.ds(pl.multiple_of(me * tokens, tokens), tokens)

    def peer_rows(o):
        return pl.ds(pl.multiple_of((me ^ o) * tokens, tokens), tokens)

    def send_in(h, o):
        return remote(
            packed.at[me ^ o, h], x_all.at[h, mine_rows], sems_in, (h, o), (dp, me ^ o)
        )

    def recv_in(h, o):
        return remote(
            packed.at[me, h], x_all.at[h, peer_rows(o)], sems_in, (h, o), (dp, me ^ o)
        )

    each(n_seq, lambda o: send_in(0, o).start(), 1)

    each(n_dp, lambda o: recv_a(o).wait_recv(), 1)
    for b in range(n_dp):
        pieces_out[b] = pieces_in[owner[b]]

    def send_b(o):
        return remote(pieces_out.at[dp ^ o], pieces_got.at[dp], sems_b, (o,), (dp ^ o, me))

    def recv_b(o):
        return remote(pieces_out.at[dp], pieces_got.at[dp ^ o], sems_b, (o,), (dp ^ o, me))

    each(n_dp, lambda o: send_b(o).start(), 1)
    pieces_got[dp] = pieces_out[dp]

    text_cot[...] = jnp.zeros_like(text_cot)
    text_cot[:, 0:txt] = cot_text[...]
    if nq > n_x:
        xt[:, n_x:nq] = jnp.zeros((256, nq - n_x), bf16)
    seen = lax.broadcasted_iota(jnp.int32, bias.shape, 0) < length[dp]
    bias[...] = jnp.where(seen, 0.0, -1e30)
    drop_clip, drop_t5 = dropped[0, dp], dropped[1, dp]

    each(n_dp, lambda o: recv_b(o).wait_recv(), 1)
    for t, (r, c) in enumerate(tiles):
        got = pieces_got[t // per, t % per].astype(f32)
        token = lax.broadcasted_iota(jnp.int32, (16, 128), 1) + c
        drop = jnp.where(token < CLIP, drop_clip, drop_t5)
        own = null_pad[r : r + 16, c : c + 128].astype(f32)
        at = pl.ds(pl.multiple_of(me * depth + r, 16), 16)
        rows_t[at, c : c + 128] = jnp.where(drop == 1, own, got).astype(bf16)

    def block(s):
        return rows_t.at[pl.ds(pl.multiple_of(s * depth, 16), depth)]

    def send_c(o):
        return remote(block(me), block(me), sems_c, (o,), (dp, me ^ o))

    def recv_c(o):
        return remote(block(me), block(me ^ o), sems_c, (o,), (dp, me ^ o))

    def send_f(o):
        return remote(block(me ^ o), block(me ^ o), sems_f, (o,), (dp, me ^ 1))

    def recv_f(o):
        return remote(block(me ^ 1), block(me ^ 1 ^ o), sems_f, (o,), (dp, me ^ 1))

    far = sorted(range(2, n_seq, 2), key=lambda o: o == n_seq // 2)
    for o in far[::-1] + [1]:
        send_c(o).start()
    def pack_rest(i):
        for j in (1, 3, 4):
            pack(i * heads + j)

    each(n_seq // 2, pack_rest)
    for h in range(1, heads):
        each(n_seq, lambda o: send_in(h, o).start(), 1)

    def own_image(h):
        x_all[h, mine_rows, :] = packed[me, h]

    each(heads, own_image)
    for o in far:
        recv_c(o).wait_recv()
        send_f(o).start()
    recv_c(1).wait_recv()
    for o in far:
        recv_f(o).wait_recv()
    w_copy.wait()
    half = w_t.shape[0] // 2
    for r in range(0, w_t.shape[0], half):
        text_qkv[r : r + half, :] = dot(w_t[r : r + half, :], rows_t[...]).astype(bf16)

    def send_out(h, o):
        return remote(
            out_all.at[h, peer_rows(o)], back.at[h, me], sems_out, (h, o), (dp, me ^ o)
        )

    def recv_out(h, o):
        return remote(
            out_all.at[h, mine_rows], back.at[h, me ^ o], sems_out, (h, o), (dp, me ^ o)
        )

    def ranges(g, side):
        lo, hi = GROUPS[g][side]
        return pl.ds(lo, hi - lo)

    def along(side, o):
        return (mx * ny + (my ^ o), me) if side == 0 else ((mx ^ o) * ny + my, me)

    def first(g, side, o, sending):
        here = my if side == 0 else mx
        other = here ^ o
        to = other if sending else here
        lane = ranges(g, side)
        src = term.at[:, to, :, lane] if side == 0 else term.at[to, :, :, lane]
        slot = here if sending else other
        return remote(
            src, term_in.at[side, slot, :, :, lane], sems_1, (g, side, o), along(side, o)
        )

    def second(g, side, o, sending):
        here = mx if side == 0 else my
        other = here ^ o
        lane = ranges(g, side)
        to = other if sending else here
        slot = here if sending else other
        return remote(
            part.at[to, :, lane],
            part_in.at[slot, :, lane],
            sems_2,
            (g, side, o),
            along(1 - side, o),
        )

    def sides_of(g):
        return [side for side in range(2) if GROUPS[g][side] is not None]

    def finish_heads(g):
        sides = sides_of(g)
        lo, hi = GROUPS[g][sides[0]][0], GROUPS[g][sides[-1]][1]
        a1, b1 = [out_all[g, img:nk, c : c + 128] for c in (0, 128)]
        low = low_lanes(a1.shape)
        if g % 2:
            b0 = out_all[g - 1, img:nk, 128:256]
            d_text[:, lo : lo + 128] = jnp.where(low, swap_halves(b0), swap_halves(a1))
            d_text[:, lo + 128 : lo + 256] = b1
        else:
            rb = swap_halves(b1)
            d_text[:, lo : lo + 128] = jnp.where(low, a1, rb)
            if hi - lo > 128:
                d_text[:, lo + 128 : hi] = jnp.where(low, rb, jnp.zeros_like(rb))
        run = 4 * chunk_rows

        def multiply(x):
            a = rows_t[pl.ds(pl.multiple_of(x * run, 16), run), 0:txt_pad]
            d = dot(a, d_text[:, lo:hi])
            pad = jnp.zeros((term.shape[2] - chunk_rows, hi - lo), f32)
            for j in range(4):
                v = jnp.concatenate([d[j * chunk_rows : (j + 1) * chunk_rows], pad], 0)
                i = 4 * x + j
                term[i // ny, i % ny, :, lo:hi] = v.astype(bf16)

        each(nx * ny // 4, multiply)
        for side in sides_of(g):
            for o in range(1, ny if side == 0 else nx):
                first(g, side, o, True).start()

    def add_first(g):
        for side in sides_of(g):
            k = ny if side == 0 else nx
            for o in range(1, k):
                first(g, side, o, False).wait_recv()
            here = my if side == 0 else mx
            lane = ranges(g, side)

            def add(j):
                own = term[j, here, :, lane] if side == 0 else term[here, j, :, lane]
                total = own.astype(f32)
                for o in range(1, k):
                    total = total + term_in[side, here ^ o, j, :, lane].astype(f32)
                part[j, :, lane] = total.astype(bf16)

            n = nx if side == 0 else ny
            each(n, add)
            for o in range(1, n):
                second(g, side, o, True).start()

    def add_second(g):
        for side in sides_of(g):
            n = nx if side == 0 else ny
            for o in range(1, n):
                second(g, side, o, False).wait_recv()
            here = mx if side == 0 else my
            lane = ranges(g, side)
            total = part[here, :, lane].astype(f32)
            for o in range(1, n):
                total = total + part_in[here ^ o, :, lane].astype(f32)
            size = min(lane.start + lane.size, d_w.shape[1]) - lane.start
            d_w[:, lane.start : lane.start + size] = total[0:chunk_rows, 0:size]

    def one_head(h):
        wide = 3 * HD
        w_rows = pl.ds(pl.multiple_of(h * wide, HD), wide)
        xt[0:wide, img:n_x] = text_qkv[w_rows, :]
        head_rows = pl.ds(pl.multiple_of(h * HD, HD), HD)
        xt[wide:256, img:n_x] = text_cot[head_rows, :]
        x, out = x_all.at[h], out_all.at[h]
        x[img:n_x, :] = xt[:, img:n_x].T
        acc[...] = jnp.zeros_like(acc)
        each(n_seq, lambda o: recv_in(h, o).wait_recv(), 1)
        for r in range(0, img, BQ):
            xt[:, r : r + BQ] = x[r : r + BQ, :].T
        all_blocks(
            nq // BQ, img, nk, x, xt, bias, s_scr, e_scrs, states, acc, out, attended_t
        )
        for k, n in chunks(nk, KC):
            out[k : k + n, 128:256] = acc[k : k + n, :].astype(bf16)
        each(n_seq, lambda o: send_out(h, o).start(), 1)
        back[h, me] = out[mine_rows, :]
        text_out[head_rows, :] = attended_t[:, img : img + txt]
        for g in range(len(GROUPS)):
            pl.when(h == g)(functools.partial(finish_heads, g))
        for g in range(len(GROUPS)):
            if g + 2 < len(GROUPS):
                pl.when(h == g + 2)(functools.partial(add_second, g))
            if g + 1 < len(GROUPS):
                pl.when(h == g + 1)(functools.partial(add_first, g))

    each(heads, one_head)

    add_second(len(GROUPS) - 2)
    add_first(len(GROUPS) - 1)
    for h in range(heads):
        each(n_seq, lambda o: recv_out(h, o).wait_recv(), 1)
    add_second(len(GROUPS) - 1)

    each(n_dp, lambda o: send_a(o).wait_send(), 1)
    each(n_dp, lambda o: send_b(o).wait_send(), 1)
    for o in far + [1]:
        send_c(o).wait_send()
    for o in far:
        send_f(o).wait_send()
    for h in range(heads):
        each(n_seq, lambda o: send_in(h, o).wait_send(), 1)
        each(n_seq, lambda o: send_out(h, o).wait_send(), 1)
    for g in range(len(GROUPS)):
        for side in sides_of(g):
            for o in range(1, ny if side == 0 else nx):
                first(g, side, o, True).wait_send()
            for o in range(1, nx if side == 0 else ny):
                second(g, side, o, True).wait_send()


def unpack_kernel(back, text_in, d_w_in, img_out, text_out, d_qkv, d_w):
    heads, n_seq = back.shape[0], back.shape[1]
    for p in range(n_seq * heads // 2):
        v = []
        for j in range(2):
            s, h = divmod(2 * p + j, heads)
            v += [back[h, s, :, 0:128], back[h, s, :, 128:256]]
        t = join_pair(*v)
        for j in range(3):
            d_qkv[:, p * 384 + 128 * j : p * 384 + 128 * j + 128] = t[j]
        img_out[:, p * 128 : p * 128 + 128] = t[3]
    text_out[...] = text_in[...]
    d_w[...] = d_w_in[...]


def on_device(
    img_qkv,
    text_cache,
    null_rows,
    w_text,
    cache_owner,
    cache_row,
    dropped,
    text_length,
    d_img_out,
    d_text_out,
):
    n_dp, n_seq = lax.axis_size("dp"), lax.axis_size("seq")
    ny = 4
    nx = n_dp // ny
    txt, depth = null_rows.shape
    tokens = img_qkv.shape[1]
    width = w_text.shape[1]
    heads = width // (3 * HD)
    img = tokens * n_seq
    nk = -(-(img + txt) // 16) * 16
    nq = -(-(img + txt) // BQ) * BQ
    txt_pad = nk - img
    lanes = -(-txt // 128) * 128
    per = -(-(depth // 16 * (lanes // 128)) // n_dp)
    chunk_rows = depth * n_seq // n_dp
    chunk_pad = -(-chunk_rows // 16) * 16
    wide = -(-width // 128) * 128
    vmem = pl.BlockSpec(memory_space=pltpu.VMEM)
    smem = pl.BlockSpec(memory_space=pltpu.SMEM)
    dma = pltpu.SemaphoreType.DMA
    out_shape = (
        jax.ShapeDtypeStruct((heads, n_seq, tokens, 256), bf16),
        jax.ShapeDtypeStruct((heads * HD, txt), bf16),
        jax.ShapeDtypeStruct((chunk_rows, width), f32),
    )
    scratch = [
        pltpu.VMEM((n_seq, heads, tokens, 256), bf16),
        pltpu.VMEM((heads, img + lanes, 256), bf16),
        pltpu.VMEM((heads, nq, 256), bf16),
        pltpu.VMEM((HD, nq), bf16),
        pltpu.VMEM((width, n_seq * depth), bf16),
        pltpu.VMEM((n_seq * depth, lanes), bf16),
        pltpu.VMEM((width, lanes), bf16),
        pltpu.VMEM((heads * HD, lanes), bf16),
        pltpu.VMEM((depth, lanes), bf16),
        pltpu.VMEM((depth, lanes), bf16),
        pltpu.VMEM((n_dp, per, 16, 128), bf16),
        pltpu.VMEM((n_dp, per, 16, 128), bf16),
        pltpu.VMEM((n_dp, per, 16, 128), bf16),
        pltpu.VMEM((n_dp, per, 16, 128), bf16),
        pltpu.VMEM((txt_pad, wide), bf16),
        pltpu.VMEM((nx, ny, chunk_pad, wide), bf16),
        pltpu.VMEM((2, ny, nx, chunk_pad, wide), bf16),
        pltpu.VMEM((nx, chunk_pad, wide), bf16),
        pltpu.VMEM((nx, chunk_pad, wide), bf16),
        pltpu.VMEM((txt_pad, 128), f32),
        pltpu.VMEM((256, nq), bf16),
        pltpu.VMEM((nk, BQ), f32),
        pltpu.VMEM((nk, BQ), bf16),
        pltpu.VMEM((nk, BQ), bf16),
        pltpu.VMEM((nk, 128), f32),
        pltpu.VMEM((128, BQ), bf16),
        pltpu.VMEM((128, BQ), bf16),
        pltpu.VMEM((BQ, 128), bf16),
        pltpu.VMEM((BQ, 128), bf16),
        pltpu.VMEM((BQ, 128), bf16),
        pltpu.VMEM((BQ, 128), bf16),
        pltpu.VMEM((8, BQ), f32),
        pltpu.VMEM((8, BQ), f32),
        pltpu.VMEM((HD, BQ), bf16),
        pltpu.VMEM((HD, BQ), bf16),
        dma,
        dma((2, n_dp)),
        dma((2, n_dp)),
        dma((2, n_seq)),
        dma((2, n_seq)),
        dma((2, heads, n_seq)),
        dma((2, heads, n_seq)),
        dma((2, len(GROUPS), 2, max(nx, ny))),
        dma((2, len(GROUPS), 2, max(nx, ny))),
    ]
    back, text_out, d_w = pl.pallas_call(
        functools.partial(kernel, (n_dp, n_seq, nx, ny)),
        out_shape=out_shape,
        in_specs=[vmem, vmem, vmem, vmem, pl.BlockSpec(memory_space=pl.ANY)]
        + [smem] * 4
        + [vmem],
        out_specs=(vmem,) * 3,
        scratch_shapes=scratch,
        compiler_params=pltpu.CompilerParams(
            collective_id=0, has_side_effects=True, vmem_limit_bytes=62 * 2**20
        ),
    )(
        img_qkv[0],
        d_img_out[0],
        text_cache.transpose(0, 2, 1),
        null_rows.T,
        w_text.T,
        cache_owner,
        cache_row,
        dropped.T,
        text_length,
        d_text_out[0].T,
    )
    steps = 2
    part = tokens // steps
    whole = [pl.BlockSpec(a.shape, lambda i: (0, 0)) for a in (text_out, d_w)]
    img_out, text_out, d_qkv, d_w = pl.pallas_call(
        unpack_kernel,
        grid=(steps,),
        out_shape=(
            jax.ShapeDtypeStruct((tokens, n_seq * heads * HD), bf16),
            jax.ShapeDtypeStruct(text_out.shape, bf16),
            jax.ShapeDtypeStruct((tokens, n_seq * width), bf16),
            jax.ShapeDtypeStruct(d_w.shape, f32),
        ),
        in_specs=[pl.BlockSpec((heads, n_seq, part, 256), lambda i: (0, 0, i, 0))] + whole,
        out_specs=(
            pl.BlockSpec((part, n_seq * heads * HD), lambda i: (i, 0)),
            whole[0],
            pl.BlockSpec((part, n_seq * width), lambda i: (i, 0)),
            whole[1],
        ),
        compiler_params=pltpu.CompilerParams(vmem_limit_bytes=62 * 2**20),
    )(back, text_out, d_w)
    return (img_out[None], text_out.T[None], d_qkv[None], d_w)


def solution(mesh):
    return jax.shard_map(
        on_device,
        mesh=mesh,
        in_specs=(
            P("dp", "seq", None),
            P("dp", None, "seq"),
            P(None, "seq"),
            P(None, "seq"),
            P(),
            P(),
            P(),
            P(),
            P("dp", "seq", None),
            P("dp", None, "seq"),
        ),
        out_specs=(
            P("dp", "seq", None),
            P("dp", None, "seq"),
            P("dp", "seq", None),
            P("dp", "seq"),
        ),
        check_vma=False,
    )
```

```python
import functools

import jax
import jax.numpy as jnp
from jax import lax
from jax.experimental import pallas as pl
from jax.experimental.pallas import tpu as pltpu
from jax.sharding import PartitionSpec as P

HD = 64
CLIP = 77
BQ = 256
KC = 464
f32, bf16 = jnp.float32, jnp.bfloat16


def chunks(n, c):
    return [(s, min(c, n - s)) for s in range(0, n, c)]


def dot(a, b):
    return jnp.dot(a, b, preferred_element_type=f32)


def fold(x, op):
    parts = [x[8 * i : 8 * i + 8] for i in range(x.shape[0] // 8)]
    while len(parts) > 1:
        parts = [
            op(parts[j], parts[j + 1]) if j + 1 < len(parts) else parts[j]
            for j in range(0, len(parts), 2)
        ]
    return parts[0]


def forward_block(i, img, nk, x, xt, bias, s_scr, e_scr, state, wq=BQ):
    w_probs, w_values, w_keys, delta, attended = state
    q0 = pl.multiple_of(i * BQ, BQ)
    zeros = jnp.zeros((HD, wq), bf16)
    q_t = xt[0:64, pl.ds(q0, wq)] * bf16(0.125)
    w_scores = jnp.concatenate([zeros, q_t], 0)
    top8 = None
    for k, n in chunks(nk, KC):
        s = dot(x[k : k + n, 0:128], w_scores)
        if k + n > img:
            b = bias[max(k - img, 0) : k + n - img, :]
            b = jnp.concatenate([b] * (wq // 128), 1)
            s = s + b if k >= img else jnp.concatenate([s[: img - k], s[img - k :] + b], 0)
        s_scr[k : k + n, 0:wq] = s
        c = fold(s, jnp.maximum)
        top8 = c if top8 is None else jnp.maximum(top8, c)
        yield
    top = jnp.max(top8, 0, keepdims=True)
    sum8 = out_t = None
    for k, n in chunks(nk, KC):
        e = jnp.exp(s_scr[k : k + n, 0:wq] - top)
        c = fold(e, jnp.add)
        sum8 = c if sum8 is None else sum8 + c
        e = e.astype(bf16)
        e_scr[k : k + n, 0:wq] = e
        o = dot(xt[128:192, k : k + n], e)
        out_t = o if out_t is None else out_t + o
        yield
    cot_t = xt[192:256, pl.ds(q0, wq)].astype(f32)
    inv = 1.0 / jnp.sum(sum8, 0, keepdims=True)
    out_t = (out_t * inv).astype(bf16)
    row_delta = jnp.sum(cot_t * out_t.astype(f32), 0, keepdims=True) * inv
    cot_s = (cot_t * inv).astype(bf16)
    w_probs[:, 0:wq] = jnp.concatenate([cot_s, zeros], 0)
    w_values[0:wq, :] = jnp.concatenate([zeros, cot_s], 0).T
    w_keys[0:wq, :] = jnp.concatenate([q_t, zeros], 0).T
    delta[:, 0:wq] = jnp.broadcast_to(row_delta, (delta.shape[0], wq))
    attended[:, 0:wq] = out_t


def backward_block(i, nk, x, xt, e_scr, state, acc, out, attended_t, wq=BQ):
    w_probs, w_values, w_keys, delta, attended = state
    q0 = pl.multiple_of(i * BQ, BQ)
    row_delta = delta[0:1, 0:wq]
    dq_t = None
    for k, n in chunks(nk, KC):
        dp = dot(x[k : k + n, 128:256], w_probs[:, 0:wq])
        e = e_scr[k : k + n, 0:wq]
        ds = (e.astype(f32) * (dp - row_delta)).astype(bf16)
        d = dot(xt[64:128, k : k + n], ds)
        dq_t = d if dq_t is None else dq_t + d
        acc[k : k + n, :] += dot(ds, w_keys[0:wq, :]) + dot(e, w_values[0:wq, :])
        yield
    dq_t = (dq_t * 0.125).astype(bf16)
    out[pl.ds(q0, wq), 0:128] = jnp.concatenate([dq_t, attended[:, 0:wq]], 0).T
    attended_t[:, pl.ds(q0, wq)] = attended[:, 0:wq]


def alternate(a, b):
    live = [True, True]
    turn = 0
    while live[0] or live[1]:
        g = 1 if turn % 3 == 2 else 0
        turn += 1
        if live[g]:
            live[g] = next((a, b)[g], "end") is None


def all_blocks(n, img, nk, x, xt, bias, s_scr, e_scrs, states, acc, out, attended_t):
    last = -(-(nk - (n - 1) * BQ) // 128) * 128

    def forward(i, side, wq=BQ):
        return forward_block(i, img, nk, x, xt, bias, s_scr, e_scrs[side], states[side], wq)

    def backward(i, side, wq=BQ):
        return backward_block(
            i, nk, x, xt, e_scrs[side], states[side], acc, out, attended_t, wq
        )

    for _ in forward(0, 0):
        pass

    def body(j, c):
        alternate(forward(2 * j + 1, 1), backward(2 * j, 0))
        alternate(forward(2 * j + 2, 0), backward(2 * j + 1, 1))
        return c

    lax.fori_loop(0, n // 2 - 1, body, 0)
    alternate(forward(n - 1, 1, last), backward(n - 2, 0))
    for _ in backward(n - 1, 1, last):
        pass


def swap_halves(v):
    return jnp.concatenate([v[:, HD:], v[:, :HD]], 1)


def low_lanes(shape):
    return lax.broadcasted_iota(jnp.int32, shape, 1) < HD


def split_pair(t0, t1, t2, cot):
    low = low_lanes(t0.shape)
    r1, r2, rc = swap_halves(t1), swap_halves(t2), swap_halves(cot)
    return (t0, jnp.where(low, t1, rc)), (jnp.where(low, r1, r2), jnp.where(low, r2, cot))


def join_pair(a0, b0, a1, b1):
    low = low_lanes(a0.shape)
    ra0, rb0, ra1 = swap_halves(a0), swap_halves(b0), swap_halves(a1)
    return (
        jnp.where(low, a0, rb0),
        jnp.where(low, rb0, ra1),
        b1,
        jnp.where(low, ra0, a1),
    )


def tiles_of(rows, lanes):
    return [(r, c) for r in range(0, rows, 16) for c in range(0, lanes, 128)]


GROUPS = (
    ((0, 128), None),
    ((128, 256), (256, 384)),
    (None, (384, 512)),
    ((512, 640), (640, 768)),
    ((768, 896), (896, 1024)),
)


def kernel(
    dims,
    qkv_hbm,
    cot_img_hbm,
    cache_hbm,
    null_rows,
    w_hbm,
    owner,
    cache_row,
    dropped,
    length,
    cot_text,
    back,
    text_out,
    d_w,
    packed,
    x_all,
    out_all,
    attended_t,
    w_t,
    rows_t,
    text_qkv,
    text_cot,
    raw,
    null_pad,
    pieces,
    pieces_in,
    pieces_out,
    pieces_got,
    d_text,
    term,
    term_in,
    part,
    part_in,
    bias,
    xt,
    s_scr,
    e_scr0,
    e_scr1,
    acc,
    st_a0,
    st_a1,
    st_b0,
    st_b1,
    st_c0,
    st_c1,
    st_d0,
    st_d1,
    st_e0,
    st_e1,
    qkv,
    cot_img,
    cache,
    sem_w,
    sems_own,
    sems_a,
    sems_b,
    sems_c,
    sems_f,
    sems_in,
    sems_out,
    sems_1,
    sems_2,
):
    n_dp, n_seq, nx, ny = dims
    dp, me = lax.axis_index("dp"), lax.axis_index("seq")
    mx, my = dp // ny, dp % ny
    tokens = qkv.shape[0]
    heads = x_all.shape[0]
    nq = xt.shape[1]
    n_x = x_all.shape[1]
    img = tokens * n_seq
    nk = e_scr0.shape[0]
    e_scrs = (e_scr0, e_scr1)
    states = ((st_a0, st_b0, st_c0, st_d0, st_e0), (st_a1, st_b1, st_c1, st_d1, st_e1))
    txt_pad = nk - img
    depth, txt = null_rows.shape
    lanes = raw.shape[1]
    per = pieces.shape[1]
    chunk_rows = d_w.shape[0]

    def remote(src, dst, sems, at, dev):
        return pltpu.make_async_remote_copy(
            src_ref=src,
            dst_ref=dst,
            send_sem=sems.at[(0,) + at],
            recv_sem=sems.at[(1,) + at],
            device_id=dev,
            device_id_type=pl.DeviceIdType.MESH,
        )

    def each(n, fn, start=0):
        def body(i, c):
            fn(i)
            return c

        lax.fori_loop(start, n, body, 0)

    barrier = pltpu.get_barrier_semaphore()

    def greet_seq(o):
        pl.semaphore_signal(
            barrier, inc=1, device_id=(dp, me ^ o), device_id_type=pl.DeviceIdType.MESH
        )

    def greet_dp(o):
        pl.semaphore_signal(
            barrier, inc=1, device_id=(dp ^ o, me), device_id_type=pl.DeviceIdType.MESH
        )

    each(n_seq, greet_seq, 1)
    each(n_dp, greet_dp, 1)
    w_copy = pltpu.make_async_copy(w_hbm, w_t, sem_w)
    cache_copy = pltpu.make_async_copy(cache_hbm, cache, sems_own.at[0])
    qkv_copy = pltpu.make_async_copy(qkv_hbm, qkv, sems_own.at[1])
    cot_copy = pltpu.make_async_copy(cot_img_hbm, cot_img, sems_own.at[2])
    for c in (cache_copy, qkv_copy, cot_copy):
        c.start()

    mine = jnp.int32(0)
    for b in range(n_dp):
        mine = jnp.where(owner[b] == dp, jnp.int32(b), mine)
    row = cache_row[mine]
    raw[...] = jnp.zeros_like(raw)
    cache_copy.wait()
    raw[:, 0:txt] = cache[row]
    null_pad[...] = jnp.zeros_like(null_pad)
    null_pad[:, 0:txt] = null_rows[...]
    tiles = tiles_of(depth, lanes)
    for t, (r, c) in enumerate(tiles):
        pieces[t // per, t % per] = raw[r : r + 16, c : c + 128]
    for t in range(len(tiles), n_dp * per):
        pieces[t // per, t % per] = jnp.zeros((16, 128), bf16)
    pieces_in[dp] = pieces[dp]

    def pack(p):
        c = pl.multiple_of(p * 384, 128)
        t = [qkv[:, pl.ds(pl.multiple_of(c + 128 * j, 128), 128)] for j in range(3)]
        g = cot_img[:, pl.ds(pl.multiple_of(p * 128, 128), 128)]
        for j, (a, b) in enumerate(split_pair(*t, g)):
            head = 2 * p + j
            to, h = head // heads, head % heads
            packed[to, h, :, 0:128] = a
            packed[to, h, :, 128:256] = b

    qkv_copy.wait()
    cot_copy.wait()
    w_copy.start()
    lax.fori_loop(0, n_seq, lambda i, c: (pack(i * heads // 2), c)[1], 0, unroll=2)

    pl.semaphore_wait(barrier, n_seq + n_dp - 2)

    def send_a(o):
        return remote(pieces.at[dp ^ o], pieces_in.at[dp], sems_a, (o,), (dp ^ o, me))

    def recv_a(o):
        return remote(pieces.at[dp], pieces_in.at[dp ^ o], sems_a, (o,), (dp ^ o, me))

    each(n_dp, lambda o: send_a(o).start(), 1)

    mine_rows = pl.ds(pl.multiple_of(me * tokens, tokens), tokens)

    def peer_rows(o):
        return pl.ds(pl.multiple_of((me ^ o) * tokens, tokens), tokens)

    def send_in(h, o):
        return remote(
            packed.at[me ^ o, h], x_all.at[h, mine_rows], sems_in, (h, o), (dp, me ^ o)
        )

    def recv_in(h, o):
        return remote(
            packed.at[me, h], x_all.at[h, peer_rows(o)], sems_in, (h, o), (dp, me ^ o)
        )

    each(n_seq, lambda o: send_in(0, o).start(), 1)

    each(n_dp, lambda o: recv_a(o).wait_recv(), 1)
    for b in range(n_dp):
        pieces_out[b] = pieces_in[owner[b]]

    def send_b(o):
        return remote(pieces_out.at[dp ^ o], pieces_got.at[dp], sems_b, (o,), (dp ^ o, me))

    def recv_b(o):
        return remote(pieces_out.at[dp], pieces_got.at[dp ^ o], sems_b, (o,), (dp ^ o, me))

    each(n_dp, lambda o: send_b(o).start(), 1)
    pieces_got[dp] = pieces_out[dp]

    text_cot[...] = jnp.zeros_like(text_cot)
    text_cot[:, 0:txt] = cot_text[...]
    if nq > n_x:
        xt[:, n_x:nq] = jnp.zeros((256, nq - n_x), bf16)
    seen = lax.broadcasted_iota(jnp.int32, bias.shape, 0) < length[dp]
    bias[...] = jnp.where(seen, 0.0, -1e30)
    drop_clip, drop_t5 = dropped[0, dp], dropped[1, dp]

    each(n_dp, lambda o: recv_b(o).wait_recv(), 1)
    for t, (r, c) in enumerate(tiles):
        got = pieces_got[t // per, t % per].astype(f32)
        token = lax.broadcasted_iota(jnp.int32, (16, 128), 1) + c
        drop = jnp.where(token < CLIP, drop_clip, drop_t5)
        own = null_pad[r : r + 16, c : c + 128].astype(f32)
        at = pl.ds(pl.multiple_of(me * depth + r, 16), 16)
        rows_t[at, c : c + 128] = jnp.where(drop == 1, own, got).astype(bf16)

    def block(s):
        return rows_t.at[pl.ds(pl.multiple_of(s * depth, 16), depth)]

    def send_c(o):
        return remote(block(me), block(me), sems_c, (o,), (dp, me ^ o))

    def recv_c(o):
        return remote(block(me), block(me ^ o), sems_c, (o,), (dp, me ^ o))

    def send_f(o):
        return remote(block(me ^ o), block(me ^ o), sems_f, (o,), (dp, me ^ 1))

    def recv_f(o):
        return remote(block(me ^ 1), block(me ^ 1 ^ o), sems_f, (o,), (dp, me ^ 1))

    far = sorted(range(2, n_seq, 2), key=lambda o: o == n_seq // 2)
    for o in far[::-1] + [1]:
        send_c(o).start()
    def pack_rest(i):
        for j in (1, 3, 4):
            pack(i * heads + j)

    each(n_seq // 2, pack_rest)
    for h in range(1, heads):
        each(n_seq, lambda o: send_in(h, o).start(), 1)

    def own_image(h):
        x_all[h, mine_rows, :] = packed[me, h]

    each(heads, own_image)
    for o in far:
        recv_c(o).wait_recv()
        send_f(o).start()
    recv_c(1).wait_recv()
    for o in far:
        recv_f(o).wait_recv()
    w_copy.wait()
    half = w_t.shape[0] // 2
    for r in range(0, w_t.shape[0], half):
        text_qkv[r : r + half, :] = dot(w_t[r : r + half, :], rows_t[...]).astype(bf16)

    def send_out(h, o):
        return remote(
            out_all.at[h, peer_rows(o)], back.at[h, me], sems_out, (h, o), (dp, me ^ o)
        )

    def recv_out(h, o):
        return remote(
            out_all.at[h, mine_rows], back.at[h, me ^ o], sems_out, (h, o), (dp, me ^ o)
        )

    def ranges(g, side):
        lo, hi = GROUPS[g][side]
        return pl.ds(lo, hi - lo)

    def along(side, o):
        return (mx * ny + (my ^ o), me) if side == 0 else ((mx ^ o) * ny + my, me)

    def first(g, side, o, sending):
        here = my if side == 0 else mx
        other = here ^ o
        to = other if sending else here
        lane = ranges(g, side)
        src = term.at[:, to, :, lane] if side == 0 else term.at[to, :, :, lane]
        slot = here if sending else other
        return remote(
            src, term_in.at[side, slot, :, :, lane], sems_1, (g, side, o), along(side, o)
        )

    def second(g, side, o, sending):
        here = mx if side == 0 else my
        other = here ^ o
        lane = ranges(g, side)
        to = other if sending else here
        slot = here if sending else other
        return remote(
            part.at[to, :, lane],
            part_in.at[slot, :, lane],
            sems_2,
            (g, side, o),
            along(1 - side, o),
        )

    def sides_of(g):
        return [side for side in range(2) if GROUPS[g][side] is not None]

    def finish_heads(g):
        sides = sides_of(g)
        lo, hi = GROUPS[g][sides[0]][0], GROUPS[g][sides[-1]][1]
        a1, b1 = [out_all[g, img:nk, c : c + 128] for c in (0, 128)]
        low = low_lanes(a1.shape)
        if g % 2:
            b0 = out_all[g - 1, img:nk, 128:256]
            d_text[:, lo : lo + 128] = jnp.where(low, swap_halves(b0), swap_halves(a1))
            d_text[:, lo + 128 : lo + 256] = b1
        else:
            rb = swap_halves(b1)
            d_text[:, lo : lo + 128] = jnp.where(low, a1, rb)
            if hi - lo > 128:
                d_text[:, lo + 128 : hi] = jnp.where(low, rb, jnp.zeros_like(rb))
        run = 4 * chunk_rows

        def multiply(x):
            a = rows_t[pl.ds(pl.multiple_of(x * run, 16), run), 0:txt_pad]
            d = dot(a, d_text[:, lo:hi])
            pad = jnp.zeros((term.shape[2] - chunk_rows, hi - lo), f32)
            for j in range(4):
                v = jnp.concatenate([d[j * chunk_rows : (j + 1) * chunk_rows], pad], 0)
                i = 4 * x + j
                term[i // ny, i % ny, :, lo:hi] = v.astype(bf16)

        each(nx * ny // 4, multiply)
        for side in sides_of(g):
            for o in range(1, ny if side == 0 else nx):
                first(g, side, o, True).start()

    def add_first(g):
        for side in sides_of(g):
            k = ny if side == 0 else nx
            for o in range(1, k):
                first(g, side, o, False).wait_recv()
            here = my if side == 0 else mx
            lane = ranges(g, side)

            def add(j):
                own = term[j, here, :, lane] if side == 0 else term[here, j, :, lane]
                total = own.astype(f32)
                for o in range(1, k):
                    total = total + term_in[side, here ^ o, j, :, lane].astype(f32)
                part[j, :, lane] = total.astype(bf16)

            n = nx if side == 0 else ny
            each(n, add)
            for o in range(1, n):
                second(g, side, o, True).start()

    def add_second(g):
        for side in sides_of(g):
            n = nx if side == 0 else ny
            for o in range(1, n):
                second(g, side, o, False).wait_recv()
            here = mx if side == 0 else my
            lane = ranges(g, side)
            total = part[here, :, lane].astype(f32)
            for o in range(1, n):
                total = total + part_in[here ^ o, :, lane].astype(f32)
            size = min(lane.start + lane.size, d_w.shape[1]) - lane.start
            d_w[:, lane.start : lane.start + size] = total[0:chunk_rows, 0:size]

    def one_head(h):
        wide = 3 * HD
        w_rows = pl.ds(pl.multiple_of(h * wide, HD), wide)
        xt[0:wide, img:n_x] = text_qkv[w_rows, :]
        head_rows = pl.ds(pl.multiple_of(h * HD, HD), HD)
        xt[wide:256, img:n_x] = text_cot[head_rows, :]
        x, out = x_all.at[h], out_all.at[h]
        x[img:n_x, :] = xt[:, img:n_x].T
        acc[...] = jnp.zeros_like(acc)
        each(n_seq, lambda o: recv_in(h, o).wait_recv(), 1)
        for r in range(0, img, BQ):
            xt[:, r : r + BQ] = x[r : r + BQ, :].T
        all_blocks(
            nq // BQ, img, nk, x, xt, bias, s_scr, e_scrs, states, acc, out, attended_t
        )
        for k, n in chunks(nk, KC):
            out[k : k + n, 128:256] = acc[k : k + n, :].astype(bf16)
        each(n_seq, lambda o: send_out(h, o).start(), 1)
        back[h, me] = out[mine_rows, :]
        text_out[head_rows, :] = attended_t[:, img : img + txt]
        for g in range(len(GROUPS)):
            pl.when(h == g)(functools.partial(finish_heads, g))
        for g in range(len(GROUPS)):
            if g + 2 < len(GROUPS):
                pl.when(h == g + 2)(functools.partial(add_second, g))
            if g + 1 < len(GROUPS):
                pl.when(h == g + 1)(functools.partial(add_first, g))

    each(heads, one_head)

    add_second(len(GROUPS) - 2)
    add_first(len(GROUPS) - 1)
    for h in range(heads):
        each(n_seq, lambda o: recv_out(h, o).wait_recv(), 1)
    add_second(len(GROUPS) - 1)

    each(n_dp, lambda o: send_a(o).wait_send(), 1)
    each(n_dp, lambda o: send_b(o).wait_send(), 1)
    for o in far + [1]:
        send_c(o).wait_send()
    for o in far:
        send_f(o).wait_send()
    for h in range(heads):
        each(n_seq, lambda o: send_in(h, o).wait_send(), 1)
        each(n_seq, lambda o: send_out(h, o).wait_send(), 1)
    for g in range(len(GROUPS)):
        for side in sides_of(g):
            for o in range(1, ny if side == 0 else nx):
                first(g, side, o, True).wait_send()
            for o in range(1, nx if side == 0 else ny):
                second(g, side, o, True).wait_send()


def unpack_kernel(back, text_in, d_w_in, img_out, text_out, d_qkv, d_w):
    heads, n_seq = back.shape[0], back.shape[1]
    for p in range(n_seq * heads // 2):
        v = []
        for j in range(2):
            s, h = divmod(2 * p + j, heads)
            v += [back[h, s, :, 0:128], back[h, s, :, 128:256]]
        t = join_pair(*v)
        for j in range(3):
            d_qkv[:, p * 384 + 128 * j : p * 384 + 128 * j + 128] = t[j]
        img_out[:, p * 128 : p * 128 + 128] = t[3]
    text_out[...] = text_in[...]
    d_w[...] = d_w_in[...]


def on_device(
    img_qkv,
    text_cache,
    null_rows,
    w_text,
    cache_owner,
    cache_row,
    dropped,
    text_length,
    d_img_out,
    d_text_out,
):
    n_dp, n_seq = lax.axis_size("dp"), lax.axis_size("seq")
    ny = 4
    nx = n_dp // ny
    txt, depth = null_rows.shape
    tokens = img_qkv.shape[1]
    width = w_text.shape[1]
    heads = width // (3 * HD)
    img = tokens * n_seq
    nk = -(-(img + txt) // 16) * 16
    nq = -(-(img + txt) // BQ) * BQ
    txt_pad = nk - img
    lanes = -(-txt // 128) * 128
    per = -(-(depth // 16 * (lanes // 128)) // n_dp)
    chunk_rows = depth * n_seq // n_dp
    chunk_pad = -(-chunk_rows // 16) * 16
    wide = -(-width // 128) * 128
    vmem = pl.BlockSpec(memory_space=pltpu.VMEM)
    smem = pl.BlockSpec(memory_space=pltpu.SMEM)
    hbm = pl.BlockSpec(memory_space=pl.ANY)
    dma = pltpu.SemaphoreType.DMA
    out_shape = (
        jax.ShapeDtypeStruct((heads, n_seq, tokens, 256), bf16),
        jax.ShapeDtypeStruct((heads * HD, txt), bf16),
        jax.ShapeDtypeStruct((chunk_rows, width), f32),
    )
    scratch = [
        pltpu.VMEM((n_seq, heads, tokens, 256), bf16),
        pltpu.VMEM((heads, img + lanes, 256), bf16),
        pltpu.VMEM((heads, nq, 256), bf16),
        pltpu.VMEM((HD, nq), bf16),
        pltpu.VMEM((width, n_seq * depth), bf16),
        pltpu.VMEM((n_seq * depth, lanes), bf16),
        pltpu.VMEM((width, lanes), bf16),
        pltpu.VMEM((heads * HD, lanes), bf16),
        pltpu.VMEM((depth, lanes), bf16),
        pltpu.VMEM((depth, lanes), bf16),
        pltpu.VMEM((n_dp, per, 16, 128), bf16),
        pltpu.VMEM((n_dp, per, 16, 128), bf16),
        pltpu.VMEM((n_dp, per, 16, 128), bf16),
        pltpu.VMEM((n_dp, per, 16, 128), bf16),
        pltpu.VMEM((txt_pad, wide), bf16),
        pltpu.VMEM((nx, ny, chunk_pad, wide), bf16),
        pltpu.VMEM((2, ny, nx, chunk_pad, wide), bf16),
        pltpu.VMEM((nx, chunk_pad, wide), bf16),
        pltpu.VMEM((nx, chunk_pad, wide), bf16),
        pltpu.VMEM((txt_pad, 128), f32),
        pltpu.VMEM((256, nq), bf16),
        pltpu.VMEM((nk, BQ), f32),
        pltpu.VMEM((nk, BQ), bf16),
        pltpu.VMEM((nk, BQ), bf16),
        pltpu.VMEM((nk, 128), f32),
        pltpu.VMEM((128, BQ), bf16),
        pltpu.VMEM((128, BQ), bf16),
        pltpu.VMEM((BQ, 128), bf16),
        pltpu.VMEM((BQ, 128), bf16),
        pltpu.VMEM((BQ, 128), bf16),
        pltpu.VMEM((BQ, 128), bf16),
        pltpu.VMEM((8, BQ), f32),
        pltpu.VMEM((8, BQ), f32),
        pltpu.VMEM((HD, BQ), bf16),
        pltpu.VMEM((HD, BQ), bf16),
        pltpu.VMEM(img_qkv.shape[1:], bf16),
        pltpu.VMEM(d_img_out.shape[1:], bf16),
        pltpu.VMEM((text_cache.shape[0], depth, txt), bf16),
        dma,
        dma((3,)),
        dma((2, n_dp)),
        dma((2, n_dp)),
        dma((2, n_seq)),
        dma((2, n_seq)),
        dma((2, heads, n_seq)),
        dma((2, heads, n_seq)),
        dma((2, len(GROUPS), 2, max(nx, ny))),
        dma((2, len(GROUPS), 2, max(nx, ny))),
    ]
    back, text_out, d_w = pl.pallas_call(
        functools.partial(kernel, (n_dp, n_seq, nx, ny)),
        out_shape=out_shape,
        in_specs=[hbm, hbm, hbm, vmem, hbm]
        + [smem] * 4
        + [vmem],
        out_specs=(vmem,) * 3,
        scratch_shapes=scratch,
        compiler_params=pltpu.CompilerParams(
            collective_id=0, has_side_effects=True, vmem_limit_bytes=63 * 2**20
        ),
    )(
        img_qkv[0],
        d_img_out[0],
        text_cache.transpose(0, 2, 1),
        null_rows.T,
        w_text.T,
        cache_owner,
        cache_row,
        dropped.T,
        text_length,
        d_text_out[0].T,
    )
    steps = 2
    part = tokens // steps
    whole = [pl.BlockSpec(a.shape, lambda i: (0, 0)) for a in (text_out, d_w)]
    img_out, text_out, d_qkv, d_w = pl.pallas_call(
        unpack_kernel,
        grid=(steps,),
        out_shape=(
            jax.ShapeDtypeStruct((tokens, n_seq * heads * HD), bf16),
            jax.ShapeDtypeStruct(text_out.shape, bf16),
            jax.ShapeDtypeStruct((tokens, n_seq * width), bf16),
            jax.ShapeDtypeStruct(d_w.shape, f32),
        ),
        in_specs=[pl.BlockSpec((heads, n_seq, part, 256), lambda i: (0, 0, i, 0))] + whole,
        out_specs=(
            pl.BlockSpec((part, n_seq * heads * HD), lambda i: (i, 0)),
            whole[0],
            pl.BlockSpec((part, n_seq * width), lambda i: (i, 0)),
            whole[1],
        ),
        compiler_params=pltpu.CompilerParams(vmem_limit_bytes=63 * 2**20),
    )(back, text_out, d_w)
    return (img_out[None], text_out.T[None], d_qkv[None], d_w)


def solution(mesh):
    return jax.shard_map(
        on_device,
        mesh=mesh,
        in_specs=(
            P("dp", "seq", None),
            P("dp", None, "seq"),
            P(None, "seq"),
            P(None, "seq"),
            P(),
            P(),
            P(),
            P(),
            P("dp", "seq", None),
            P("dp", None, "seq"),
        ),
        out_specs=(
            P("dp", "seq", None),
            P("dp", None, "seq"),
            P("dp", "seq", None),
            P("dp", "seq"),
        ),
        check_vma=False,
    )
```

```python
import functools

import jax
import jax.numpy as jnp
from jax import lax
from jax.experimental import pallas as pl
from jax.experimental.pallas import tpu as pltpu
from jax.sharding import PartitionSpec as P

HD = 64
CLIP = 77
BQ = 256
KC = 464
f32, bf16 = jnp.float32, jnp.bfloat16


def chunks(n, c):
    return [(s, min(c, n - s)) for s in range(0, n, c)]


def dot(a, b):
    return jnp.dot(a, b, preferred_element_type=f32)


def fold(x, op):
    parts = [x[8 * i : 8 * i + 8] for i in range(x.shape[0] // 8)]
    while len(parts) > 1:
        parts = [
            op(parts[j], parts[j + 1]) if j + 1 < len(parts) else parts[j]
            for j in range(0, len(parts), 2)
        ]
    return parts[0]


def forward_block(i, img, nk, x, xt, bias, s_scr, e_scr, state, wq=BQ):
    w_probs, w_values, w_keys, delta, attended = state
    q0 = pl.multiple_of(i * BQ, BQ)
    zeros = jnp.zeros((HD, wq), bf16)
    q_t = xt[0:64, pl.ds(q0, wq)] * bf16(0.125)
    w_scores = jnp.concatenate([zeros, q_t], 0)
    top8 = None
    for k, n in chunks(nk, KC):
        s = dot(x[k : k + n, 0:128], w_scores)
        if k + n > img:
            b = bias[max(k - img, 0) : k + n - img, :]
            b = jnp.concatenate([b] * (wq // 128), 1)
            s = s + b if k >= img else jnp.concatenate([s[: img - k], s[img - k :] + b], 0)
        s_scr[k : k + n, 0:wq] = s
        c = fold(s, jnp.maximum)
        top8 = c if top8 is None else jnp.maximum(top8, c)
        yield
    top = jnp.max(top8, 0, keepdims=True)
    sum8 = out_t = None
    for k, n in chunks(nk, KC):
        e = jnp.exp(s_scr[k : k + n, 0:wq] - top)
        c = fold(e, jnp.add)
        sum8 = c if sum8 is None else sum8 + c
        e = e.astype(bf16)
        e_scr[k : k + n, 0:wq] = e
        o = dot(xt[128:192, k : k + n], e)
        out_t = o if out_t is None else out_t + o
        yield
    cot_t = xt[192:256, pl.ds(q0, wq)].astype(f32)
    inv = 1.0 / jnp.sum(sum8, 0, keepdims=True)
    out_t = (out_t * inv).astype(bf16)
    row_delta = jnp.sum(cot_t * out_t.astype(f32), 0, keepdims=True) * inv
    cot_s = (cot_t * inv).astype(bf16)
    w_probs[:, 0:wq] = jnp.concatenate([cot_s, zeros], 0)
    w_values[0:wq, :] = jnp.concatenate([zeros, cot_s], 0).T
    w_keys[0:wq, :] = jnp.concatenate([q_t, zeros], 0).T
    delta[:, 0:wq] = jnp.broadcast_to(row_delta, (delta.shape[0], wq))
    attended[:, 0:wq] = out_t


def backward_block(i, nk, x, xt, e_scr, state, acc, out, attended_t, wq=BQ):
    w_probs, w_values, w_keys, delta, attended = state
    q0 = pl.multiple_of(i * BQ, BQ)
    row_delta = delta[0:1, 0:wq]
    dq_t = None
    for k, n in chunks(nk, KC):
        dp = dot(x[k : k + n, 128:256], w_probs[:, 0:wq])
        e = e_scr[k : k + n, 0:wq]
        ds = (e.astype(f32) * (dp - row_delta)).astype(bf16)
        d = dot(xt[64:128, k : k + n], ds)
        dq_t = d if dq_t is None else dq_t + d
        acc[k : k + n, :] += dot(ds, w_keys[0:wq, :]) + dot(e, w_values[0:wq, :])
        yield
    dq_t = (dq_t * 0.125).astype(bf16)
    out[pl.ds(q0, wq), 0:128] = jnp.concatenate([dq_t, attended[:, 0:wq]], 0).T
    attended_t[:, pl.ds(q0, wq)] = attended[:, 0:wq]


def alternate(a, b):
    live = [True, True]
    turn = 0
    while live[0] or live[1]:
        g = 1 if turn % 3 == 2 else 0
        turn += 1
        if live[g]:
            live[g] = next((a, b)[g], "end") is None


def all_blocks(n, img, nk, x, xt, bias, s_scr, e_scrs, states, acc, out, attended_t):
    last = -(-(nk - (n - 1) * BQ) // 128) * 128

    def forward(i, side, wq=BQ):
        return forward_block(i, img, nk, x, xt, bias, s_scr, e_scrs[side], states[side], wq)

    def backward(i, side, wq=BQ):
        return backward_block(
            i, nk, x, xt, e_scrs[side], states[side], acc, out, attended_t, wq
        )

    for _ in forward(0, 0):
        pass

    def body(j, c):
        alternate(forward(2 * j + 1, 1), backward(2 * j, 0))
        alternate(forward(2 * j + 2, 0), backward(2 * j + 1, 1))
        return c

    lax.fori_loop(0, n // 2 - 1, body, 0)
    alternate(forward(n - 1, 1, last), backward(n - 2, 0))
    for _ in backward(n - 1, 1, last):
        pass


def swap_halves(v):
    return jnp.concatenate([v[:, HD:], v[:, :HD]], 1)


def low_lanes(shape):
    return lax.broadcasted_iota(jnp.int32, shape, 1) < HD


def split_pair(t0, t1, t2, cot):
    low = low_lanes(t0.shape)
    r1, r2, rc = swap_halves(t1), swap_halves(t2), swap_halves(cot)
    return (t0, jnp.where(low, t1, rc)), (jnp.where(low, r1, r2), jnp.where(low, r2, cot))


def join_pair(a0, b0, a1, b1):
    low = low_lanes(a0.shape)
    ra0, rb0, ra1 = swap_halves(a0), swap_halves(b0), swap_halves(a1)
    return (
        jnp.where(low, a0, rb0),
        jnp.where(low, rb0, ra1),
        b1,
        jnp.where(low, ra0, a1),
    )


def tiles_of(rows, lanes):
    return [(r, c) for r in range(0, rows, 16) for c in range(0, lanes, 128)]


GROUPS = (
    ((0, 128), None),
    ((128, 256), (256, 384)),
    (None, (384, 512)),
    ((512, 640), (640, 768)),
    ((768, 896), (896, 1024)),
)


def kernel(
    dims,
    qkv,
    cot_img,
    cache,
    null_rows,
    w_hbm,
    owner,
    cache_row,
    dropped,
    length,
    cot_text,
    back,
    text_out,
    d_w,
    packed,
    x_all,
    out_all,
    attended_t,
    w_t,
    rows_t,
    text_qkv,
    text_cot,
    raw,
    null_pad,
    pieces,
    pieces_in,
    pieces_out,
    pieces_got,
    d_text,
    term,
    term_in,
    part,
    part_in,
    bias,
    xt,
    s_scr,
    e_scr0,
    e_scr1,
    acc,
    st_a0,
    st_a1,
    st_b0,
    st_b1,
    st_c0,
    st_c1,
    st_d0,
    st_d1,
    st_e0,
    st_e1,
    sem_w,
    sems_a,
    sems_b,
    sems_c,
    sems_f,
    sems_in,
    sems_out,
    sems_1,
    sems_2,
):
    n_dp, n_seq, nx, ny = dims
    dp, me = lax.axis_index("dp"), lax.axis_index("seq")
    mx, my = dp // ny, dp % ny
    tokens = qkv.shape[0]
    heads = x_all.shape[0]
    nq = xt.shape[1]
    n_x = x_all.shape[1]
    img = tokens * n_seq
    nk = e_scr0.shape[0]
    e_scrs = (e_scr0, e_scr1)
    states = ((st_a0, st_b0, st_c0, st_d0, st_e0), (st_a1, st_b1, st_c1, st_d1, st_e1))
    txt_pad = nk - img
    depth, txt = null_rows.shape
    lanes = raw.shape[1]
    per = pieces.shape[1]
    chunk_rows = d_w.shape[0]

    def remote(src, dst, sems, at, dev):
        return pltpu.make_async_remote_copy(
            src_ref=src,
            dst_ref=dst,
            send_sem=sems.at[(0,) + at],
            recv_sem=sems.at[(1,) + at],
            device_id=dev,
            device_id_type=pl.DeviceIdType.MESH,
        )

    def each(n, fn, start=0):
        def body(i, c):
            fn(i)
            return c

        lax.fori_loop(start, n, body, 0)

    barrier = pltpu.get_barrier_semaphore()

    def greet_seq(o):
        pl.semaphore_signal(
            barrier, inc=1, device_id=(dp, me ^ o), device_id_type=pl.DeviceIdType.MESH
        )

    def greet_dp(o):
        pl.semaphore_signal(
            barrier, inc=1, device_id=(dp ^ o, me), device_id_type=pl.DeviceIdType.MESH
        )

    each(n_seq, greet_seq, 1)
    each(n_dp, greet_dp, 1)
    w_copy = pltpu.make_async_copy(w_hbm, w_t, sem_w)
    w_copy.start()

    mine = jnp.int32(0)
    for b in range(n_dp):
        mine = jnp.where(owner[b] == dp, jnp.int32(b), mine)
    row = cache_row[mine]
    raw[...] = jnp.zeros_like(raw)
    raw[:, 0:txt] = cache[row]
    null_pad[...] = jnp.zeros_like(null_pad)
    null_pad[:, 0:txt] = null_rows[...]
    tiles = tiles_of(depth, lanes)
    for t, (r, c) in enumerate(tiles):
        pieces[t // per, t % per] = raw[r : r + 16, c : c + 128]
    for t in range(len(tiles), n_dp * per):
        pieces[t // per, t % per] = jnp.zeros((16, 128), bf16)
    pieces_in[dp] = pieces[dp]

    def pack(p):
        c = pl.multiple_of(p * 384, 128)
        t = [qkv[:, pl.ds(pl.multiple_of(c + 128 * j, 128), 128)] for j in range(3)]
        g = cot_img[:, pl.ds(pl.multiple_of(p * 128, 128), 128)]
        for j, (a, b) in enumerate(split_pair(*t, g)):
            head = 2 * p + j
            to, h = head // heads, head % heads
            packed[to, h, :, 0:128] = a
            packed[to, h, :, 128:256] = b

    lax.fori_loop(0, n_seq, lambda i, c: (pack(i * heads // 2), c)[1], 0, unroll=2)

    pl.semaphore_wait(barrier, n_seq + n_dp - 2)

    def send_a(o):
        return remote(pieces.at[dp ^ o], pieces_in.at[dp], sems_a, (o,), (dp ^ o, me))

    def recv_a(o):
        return remote(pieces.at[dp], pieces_in.at[dp ^ o], sems_a, (o,), (dp ^ o, me))

    each(n_dp, lambda o: send_a(o).start(), 1)

    mine_rows = pl.ds(pl.multiple_of(me * tokens, tokens), tokens)

    def peer_rows(o):
        return pl.ds(pl.multiple_of((me ^ o) * tokens, tokens), tokens)

    def send_in(h, o):
        return remote(
            packed.at[me ^ o, h], x_all.at[h, mine_rows], sems_in, (h, o), (dp, me ^ o)
        )

    def recv_in(h, o):
        return remote(
            packed.at[me, h], x_all.at[h, peer_rows(o)], sems_in, (h, o), (dp, me ^ o)
        )

    each(n_seq, lambda o: send_in(0, o).start(), 1)

    each(n_dp, lambda o: recv_a(o).wait_recv(), 1)
    for b in range(n_dp):
        pieces_out[b] = pieces_in[owner[b]]

    def send_b(o):
        return remote(pieces_out.at[dp ^ o], pieces_got.at[dp], sems_b, (o,), (dp ^ o, me))

    def recv_b(o):
        return remote(pieces_out.at[dp], pieces_got.at[dp ^ o], sems_b, (o,), (dp ^ o, me))

    each(n_dp, lambda o: send_b(o).start(), 1)
    pieces_got[dp] = pieces_out[dp]

    text_cot[...] = jnp.zeros_like(text_cot)
    text_cot[:, 0:txt] = cot_text[...]
    if nq > n_x:
        xt[:, n_x:nq] = jnp.zeros((256, nq - n_x), bf16)
    seen = lax.broadcasted_iota(jnp.int32, bias.shape, 0) < length[dp]
    bias[...] = jnp.where(seen, 0.0, -1e30)
    drop_clip, drop_t5 = dropped[0, dp], dropped[1, dp]

    each(n_dp, lambda o: recv_b(o).wait_recv(), 1)
    for t, (r, c) in enumerate(tiles):
        got = pieces_got[t // per, t % per].astype(f32)
        token = lax.broadcasted_iota(jnp.int32, (16, 128), 1) + c
        drop = jnp.where(token < CLIP, drop_clip, drop_t5)
        own = null_pad[r : r + 16, c : c + 128].astype(f32)
        at = pl.ds(pl.multiple_of(me * depth + r, 16), 16)
        rows_t[at, c : c + 128] = jnp.where(drop == 1, own, got).astype(bf16)

    def block(s):
        return rows_t.at[pl.ds(pl.multiple_of(s * depth, 16), depth)]

    def send_c(o):
        return remote(block(me), block(me), sems_c, (o,), (dp, me ^ o))

    def recv_c(o):
        return remote(block(me), block(me ^ o), sems_c, (o,), (dp, me ^ o))

    def send_f(o):
        return remote(block(me ^ o), block(me ^ o), sems_f, (o,), (dp, me ^ 1))

    def recv_f(o):
        return remote(block(me ^ 1), block(me ^ 1 ^ o), sems_f, (o,), (dp, me ^ 1))

    far = sorted(range(2, n_seq, 2), key=lambda o: o == n_seq // 2)
    for o in far[::-1] + [1]:
        send_c(o).start()
    def pack_rest(i):
        for j in (1, 3, 4):
            pack(i * heads + j)

    each(n_seq // 2, pack_rest)
    for h in range(1, heads):
        each(n_seq, lambda o: send_in(h, o).start(), 1)

    def own_image(h):
        x_all[h, mine_rows, :] = packed[me, h]

    each(heads, own_image)
    for o in far:
        recv_c(o).wait_recv()
        send_f(o).start()
    recv_c(1).wait_recv()
    for o in far:
        recv_f(o).wait_recv()
    w_copy.wait()
    half = w_t.shape[0] // 2
    for r in range(0, w_t.shape[0], half):
        text_qkv[r : r + half, :] = dot(w_t[r : r + half, :], rows_t[...]).astype(bf16)

    def send_out(h, o):
        return remote(
            out_all.at[h, peer_rows(o)], back.at[h, me], sems_out, (h, o), (dp, me ^ o)
        )

    def recv_out(h, o):
        return remote(
            out_all.at[h, mine_rows], back.at[h, me ^ o], sems_out, (h, o), (dp, me ^ o)
        )

    def ranges(g, side):
        lo, hi = GROUPS[g][side]
        return pl.ds(lo, hi - lo)

    def along(side, o):
        return (mx * ny + (my ^ o), me) if side == 0 else ((mx ^ o) * ny + my, me)

    def first(g, side, o, sending):
        here = my if side == 0 else mx
        other = here ^ o
        to = other if sending else here
        lane = ranges(g, side)
        src = term.at[:, to, :, lane] if side == 0 else term.at[to, :, :, lane]
        slot = here if sending else other
        return remote(
            src, term_in.at[side, slot, :, :, lane], sems_1, (g, side, o), along(side, o)
        )

    def second(g, side, o, sending):
        here = mx if side == 0 else my
        other = here ^ o
        lane = ranges(g, side)
        to = other if sending else here
        slot = here if sending else other
        return remote(
            part.at[to, :, lane],
            part_in.at[slot, :, lane],
            sems_2,
            (g, side, o),
            along(1 - side, o),
        )

    def sides_of(g):
        return [side for side in range(2) if GROUPS[g][side] is not None]

    def finish_heads(g):
        sides = sides_of(g)
        lo, hi = GROUPS[g][sides[0]][0], GROUPS[g][sides[-1]][1]
        a1, b1 = [out_all[g, img:nk, c : c + 128] for c in (0, 128)]
        low = low_lanes(a1.shape)
        if g % 2:
            b0 = out_all[g - 1, img:nk, 128:256]
            d_text[:, lo : lo + 128] = jnp.where(low, swap_halves(b0), swap_halves(a1))
            d_text[:, lo + 128 : lo + 256] = b1
        else:
            rb = swap_halves(b1)
            d_text[:, lo : lo + 128] = jnp.where(low, a1, rb)
            if hi - lo > 128:
                d_text[:, lo + 128 : hi] = jnp.where(low, rb, jnp.zeros_like(rb))
        run = 4 * chunk_rows

        def multiply(x):
            a = rows_t[pl.ds(pl.multiple_of(x * run, 16), run), 0:txt_pad]
            d = dot(a, d_text[:, lo:hi])
            pad = jnp.zeros((term.shape[2] - chunk_rows, hi - lo), f32)
            for j in range(4):
                v = jnp.concatenate([d[j * chunk_rows : (j + 1) * chunk_rows], pad], 0)
                i = 4 * x + j
                term[i // ny, i % ny, :, lo:hi] = v.astype(bf16)

        each(nx * ny // 4, multiply)
        for side in sides_of(g):
            for o in range(1, ny if side == 0 else nx):
                first(g, side, o, True).start()

    def add_first(g):
        for side in sides_of(g):
            k = ny if side == 0 else nx
            for o in range(1, k):
                first(g, side, o, False).wait_recv()
            here = my if side == 0 else mx
            lane = ranges(g, side)

            def add(j):
                own = term[j, here, :, lane] if side == 0 else term[here, j, :, lane]
                total = own.astype(f32)
                for o in range(1, k):
                    total = total + term_in[side, here ^ o, j, :, lane].astype(f32)
                part[j, :, lane] = total.astype(bf16)

            n = nx if side == 0 else ny
            each(n, add)
            for o in range(1, n):
                second(g, side, o, True).start()

    def add_second(g):
        for side in sides_of(g):
            n = nx if side == 0 else ny
            for o in range(1, n):
                second(g, side, o, False).wait_recv()
            here = mx if side == 0 else my
            lane = ranges(g, side)
            total = part[here, :, lane].astype(f32)
            for o in range(1, n):
                total = total + part_in[here ^ o, :, lane].astype(f32)
            size = min(lane.start + lane.size, d_w.shape[1]) - lane.start
            d_w[:, lane.start : lane.start + size] = total[0:chunk_rows, 0:size]

    def one_head(h):
        wide = 3 * HD
        w_rows = pl.ds(pl.multiple_of(h * wide, HD), wide)
        xt[0:wide, img:n_x] = text_qkv[w_rows, :]
        head_rows = pl.ds(pl.multiple_of(h * HD, HD), HD)
        xt[wide:256, img:n_x] = text_cot[head_rows, :]
        x, out = x_all.at[h], out_all.at[h]
        x[img:n_x, :] = xt[:, img:n_x].T
        acc[...] = jnp.zeros_like(acc)
        each(n_seq, lambda o: recv_in(h, o).wait_recv(), 1)
        for r in range(0, img, BQ):
            xt[:, r : r + BQ] = x[r : r + BQ, :].T
        all_blocks(
            nq // BQ, img, nk, x, xt, bias, s_scr, e_scrs, states, acc, out, attended_t
        )
        for k, n in chunks(nk, KC):
            out[k : k + n, 128:256] = acc[k : k + n, :].astype(bf16)
        for g in range(len(GROUPS)):
            pl.when(h == g)(functools.partial(finish_heads, g))
        each(n_seq, lambda o: send_out(h, o).start(), 1)
        back[h, me] = out[mine_rows, :]
        text_out[head_rows, :] = attended_t[:, img : img + txt]
        for g in range(len(GROUPS)):
            if g + 2 < len(GROUPS):
                pl.when(h == g + 2)(functools.partial(add_second, g))
            if g + 1 < len(GROUPS):
                pl.when(h == g + 1)(functools.partial(add_first, g))

    each(heads, one_head)

    add_second(len(GROUPS) - 2)
    add_first(len(GROUPS) - 1)
    for h in range(heads):
        each(n_seq, lambda o: recv_out(h, o).wait_recv(), 1)
    add_second(len(GROUPS) - 1)

    each(n_dp, lambda o: send_a(o).wait_send(), 1)
    each(n_dp, lambda o: send_b(o).wait_send(), 1)
    for o in far + [1]:
        send_c(o).wait_send()
    for o in far:
        send_f(o).wait_send()
    for h in range(heads):
        each(n_seq, lambda o: send_in(h, o).wait_send(), 1)
        each(n_seq, lambda o: send_out(h, o).wait_send(), 1)
    for g in range(len(GROUPS)):
        for side in sides_of(g):
            for o in range(1, ny if side == 0 else nx):
                first(g, side, o, True).wait_send()
            for o in range(1, nx if side == 0 else ny):
                second(g, side, o, True).wait_send()


def unpack_kernel(back, text_in, d_w_in, img_out, text_out, d_qkv, d_w):
    heads, n_seq = back.shape[0], back.shape[1]
    for p in range(n_seq * heads // 2):
        v = []
        for j in range(2):
            s, h = divmod(2 * p + j, heads)
            v += [back[h, s, :, 0:128], back[h, s, :, 128:256]]
        t = join_pair(*v)
        for j in range(3):
            d_qkv[:, p * 384 + 128 * j : p * 384 + 128 * j + 128] = t[j]
        img_out[:, p * 128 : p * 128 + 128] = t[3]
    text_out[...] = text_in[...]
    d_w[...] = d_w_in[...]


def on_device(
    img_qkv,
    text_cache,
    null_rows,
    w_text,
    cache_owner,
    cache_row,
    dropped,
    text_length,
    d_img_out,
    d_text_out,
):
    n_dp, n_seq = lax.axis_size("dp"), lax.axis_size("seq")
    ny = 4
    nx = n_dp // ny
    txt, depth = null_rows.shape
    tokens = img_qkv.shape[1]
    width = w_text.shape[1]
    heads = width // (3 * HD)
    img = tokens * n_seq
    nk = -(-(img + txt) // 16) * 16
    nq = -(-(img + txt) // BQ) * BQ
    txt_pad = nk - img
    lanes = -(-txt // 128) * 128
    per = -(-(depth // 16 * (lanes // 128)) // n_dp)
    chunk_rows = depth * n_seq // n_dp
    chunk_pad = -(-chunk_rows // 16) * 16
    wide = -(-width // 128) * 128
    vmem = pl.BlockSpec(memory_space=pltpu.VMEM)
    smem = pl.BlockSpec(memory_space=pltpu.SMEM)
    dma = pltpu.SemaphoreType.DMA
    out_shape = (
        jax.ShapeDtypeStruct((heads, n_seq, tokens, 256), bf16),
        jax.ShapeDtypeStruct((heads * HD, txt), bf16),
        jax.ShapeDtypeStruct((chunk_rows, width), f32),
    )
    scratch = [
        pltpu.VMEM((n_seq, heads, tokens, 256), bf16),
        pltpu.VMEM((heads, img + lanes, 256), bf16),
        pltpu.VMEM((heads, nq, 256), bf16),
        pltpu.VMEM((HD, nq), bf16),
        pltpu.VMEM((width, n_seq * depth), bf16),
        pltpu.VMEM((n_seq * depth, lanes), bf16),
        pltpu.VMEM((width, lanes), bf16),
        pltpu.VMEM((heads * HD, lanes), bf16),
        pltpu.VMEM((depth, lanes), bf16),
        pltpu.VMEM((depth, lanes), bf16),
        pltpu.VMEM((n_dp, per, 16, 128), bf16),
        pltpu.VMEM((n_dp, per, 16, 128), bf16),
        pltpu.VMEM((n_dp, per, 16, 128), bf16),
        pltpu.VMEM((n_dp, per, 16, 128), bf16),
        pltpu.VMEM((txt_pad, wide), bf16),
        pltpu.VMEM((nx, ny, chunk_pad, wide), bf16),
        pltpu.VMEM((2, ny, nx, chunk_pad, wide), bf16),
        pltpu.VMEM((nx, chunk_pad, wide), bf16),
        pltpu.VMEM((nx, chunk_pad, wide), bf16),
        pltpu.VMEM((txt_pad, 128), f32),
        pltpu.VMEM((256, nq), bf16),
        pltpu.VMEM((nk, BQ), f32),
        pltpu.VMEM((nk, BQ), bf16),
        pltpu.VMEM((nk, BQ), bf16),
        pltpu.VMEM((nk, 128), f32),
        pltpu.VMEM((128, BQ), bf16),
        pltpu.VMEM((128, BQ), bf16),
        pltpu.VMEM((BQ, 128), bf16),
        pltpu.VMEM((BQ, 128), bf16),
        pltpu.VMEM((BQ, 128), bf16),
        pltpu.VMEM((BQ, 128), bf16),
        pltpu.VMEM((8, BQ), f32),
        pltpu.VMEM((8, BQ), f32),
        pltpu.VMEM((HD, BQ), bf16),
        pltpu.VMEM((HD, BQ), bf16),
        dma,
        dma((2, n_dp)),
        dma((2, n_dp)),
        dma((2, n_seq)),
        dma((2, n_seq)),
        dma((2, heads, n_seq)),
        dma((2, heads, n_seq)),
        dma((2, len(GROUPS), 2, max(nx, ny))),
        dma((2, len(GROUPS), 2, max(nx, ny))),
    ]
    back, text_out, d_w = pl.pallas_call(
        functools.partial(kernel, (n_dp, n_seq, nx, ny)),
        out_shape=out_shape,
        in_specs=[vmem, vmem, vmem, vmem, pl.BlockSpec(memory_space=pl.ANY)]
        + [smem] * 4
        + [vmem],
        out_specs=(vmem,) * 3,
        scratch_shapes=scratch,
        compiler_params=pltpu.CompilerParams(
            collective_id=0, has_side_effects=True, vmem_limit_bytes=62 * 2**20
        ),
    )(
        img_qkv[0],
        d_img_out[0],
        text_cache.transpose(0, 2, 1),
        null_rows.T,
        w_text.T,
        cache_owner,
        cache_row,
        dropped.T,
        text_length,
        d_text_out[0].T,
    )
    steps = 2
    part = tokens // steps
    whole = [pl.BlockSpec(a.shape, lambda i: (0, 0)) for a in (text_out, d_w)]
    img_out, text_out, d_qkv, d_w = pl.pallas_call(
        unpack_kernel,
        grid=(steps,),
        out_shape=(
            jax.ShapeDtypeStruct((tokens, n_seq * heads * HD), bf16),
            jax.ShapeDtypeStruct(text_out.shape, bf16),
            jax.ShapeDtypeStruct((tokens, n_seq * width), bf16),
            jax.ShapeDtypeStruct(d_w.shape, f32),
        ),
        in_specs=[pl.BlockSpec((heads, n_seq, part, 256), lambda i: (0, 0, i, 0))] + whole,
        out_specs=(
            pl.BlockSpec((part, n_seq * heads * HD), lambda i: (i, 0)),
            whole[0],
            pl.BlockSpec((part, n_seq * width), lambda i: (i, 0)),
            whole[1],
        ),
        compiler_params=pltpu.CompilerParams(vmem_limit_bytes=62 * 2**20),
    )(back, text_out, d_w)
    return (img_out[None], text_out.T[None], d_qkv[None], d_w)


def solution(mesh):
    return jax.shard_map(
        on_device,
        mesh=mesh,
        in_specs=(
            P("dp", "seq", None),
            P("dp", None, "seq"),
            P(None, "seq"),
            P(None, "seq"),
            P(),
            P(),
            P(),
            P(),
            P("dp", "seq", None),
            P("dp", None, "seq"),
        ),
        out_specs=(
            P("dp", "seq", None),
            P("dp", None, "seq"),
            P("dp", "seq", None),
            P("dp", "seq"),
        ),
        check_vma=False,
    )
```
